32 devices in a mesh: groups: 2 (over x), dp: 16 (over z, y, core).
Axes of the slice: x: 2, y: 2, z: 4, core: 2. Of those that a mesh axis runs over, the one named last changes fastest.
Arguments:
- queries: bfloat16 [16384, 1024], P(('groups', 'dp')), parts along dimension 0, may hold values from -5.5 to 5.5
- kv_cache: bfloat16 [16384, 256], P(('groups', 'dp')), parts along dimension 0, may hold values from -5.5 to 5.5
- grad_out: bfloat16 [16384, 1024], P(('groups', 'dp')), parts along dimension 0, may hold values from -48 to 48
- pair_lengths: int32 [20], P('groups'), parts along dimension 0, may hold values from 1 to 12, 32 in all
Outputs:
- grad_queries: bfloat16 [16384, 1024], P(('groups', 'dp')), parts along dimension 0
- grad_kv: float32 [16384, 256], P(('groups', 'dp')), parts along dimension 0
The draws below stay inside these ranges and needn't reach their ends.
There are 2 independent parts, one for each index of `groups`. The reference program is written for one: setup_inputs(seed, part) draws one part's arguments, and reference() takes and returns one part's arrays. A program takes and returns all parts, laid end to end along the dimension named above; each array names one. Nothing has to cross between parts.
Inputs may be any that keep to these rules, and one draw needn't show every extreme that they name: `pair_lengths`: the 10 lengths sum to 32; the longest is exactly 12.
All inputs are finite; a program needn't handle non-finite values.
Results may differ from the reference program's by a relative error of at most 0.0078.
Values may be sent and summed in bfloat16 or wider, within the bound.
No kernel may reach another device: no remote copies, remote signals or barrier semaphores. Data moves between devices by JAX's collectives and lax.ppermute only.
A program may use at most 192 MiB of HBM per device.

```python
import math
import jax
import jax.numpy as jnp
import numpy as np
from jax import lax

HD = 128
QH = 8
TILE = 256
MOST = 12
TOKENS = 8192
TILES_ALL = 32
NPAIRS = 10


def draw_queries(key, part):
    result = jnp.clip(jax.random.normal(jax.random.fold_in(key, 31), (TOKENS, QH * HD), jnp.float32), -5.5, 5.5)
    return result.astype(jnp.bfloat16)


def draw_kv_cache(key, part):
    key_part = jnp.clip(jax.random.normal(jax.random.fold_in(key, 21), (TOKENS, HD), jnp.float32), -5.5, 5.5)
    value_part = jnp.clip(jax.random.normal(jax.random.fold_in(key, 22), (TOKENS, HD), jnp.float32), -5.5, 5.5)
    return jnp.concatenate([key_part, value_part], axis=1).astype(jnp.bfloat16)


def shard_levels(key, dims, shards, low, largest):
    level, own = 1.0, jax.random.fold_in(key, 6)
    for dim, blocks in shards:
        draws = jnp.exp(jax.random.uniform(jax.random.fold_in(own, dim), (blocks,), jnp.float32, low / len(shards), largest / len(shards)))
        level = level * jnp.repeat(draws, dims[dim] // blocks).reshape([-1 if axis == dim else 1 for axis in range(len(dims))])
    return level


def profile(amount, total, reach, lean):
    portions = [(1 << 20) // math.isqrt(grade ** lean) + 1 for grade in range(2, amount + 1)]
    spare, given = total - reach - (amount - 1), [1] * (amount - 1)
    while spare > 0:
        candidates = [i for i in range(amount - 1) if given[i] < reach]
        whole, left = sum([portions[i] for i in candidates]), spare
        for i in candidates:
            addition = min(reach - given[i], max(1, left * portions[i] // whole), spare)
            given[i] = given[i] + addition
            spare = spare - addition
    return np.array([reach] + given)


def ragged_sizes(key, amount, total, most, lean):
    if amount == 2:
        one = jax.random.randint(key, (), max(1, total - most), min(most, total - 1) + 1)
        return jnp.stack([one, total - one])
    lengths = jnp.asarray(profile(amount, total, most, lean), jnp.int32)
    pairs = (amount - 1) // 2
    giver, taker = lengths[1:1 + 2 * pairs:2], lengths[2:2 + 2 * pairs:2]
    margin = jnp.minimum(giver - 1, most - taker)
    passed = jax.random.randint(jax.random.fold_in(key, 1), (pairs,), 0, 1 << 20) % (margin + 1)
    lengths = lengths.at[1:1 + 2 * pairs:2].set(giver - passed).at[2:2 + 2 * pairs:2].set(taker + passed)
    return lengths[jax.random.permutation(jax.random.fold_in(key, 2), amount)]


def scatter_about(key, dims, width, bound, shards=(), kind=jnp.bfloat16):
    values = jax.random.normal(key, dims, jnp.float32) * width
    if len(shards) > 0:
        values = shard_levels(key, dims, shards, -0.22, 0.18) * values
    return jnp.clip(values, min=-bound, max=bound).astype(kind)


def setup_inputs(seed: int = 0, part: int = 0) -> dict:
    arg_keys = jax.random.split(jax.random.key(seed), 5)
    part_splits = jax.random.split(jax.random.fold_in(arg_keys[4], part), 5)
    queries = draw_queries(jax.random.fold_in(jax.random.fold_in(arg_keys[4], part), 71), part)
    kv_cache = draw_kv_cache(jax.random.fold_in(jax.random.fold_in(arg_keys[4], part), 71), part)
    grad_out = scatter_about(part_splits[2], (TOKENS, QH * HD), 8.0, 48.0, ((0, 16),))
    pair_lengths = ragged_sizes(part_splits[3], NPAIRS, TILES_ALL, MOST, 2).astype(jnp.int32)
    return dict(queries=queries, kv_cache=kv_cache, grad_out=grad_out, pair_lengths=pair_lengths)


def pair_span(pair_lengths, tile_index):
    pair_ends = jnp.cumsum(pair_lengths).astype(jnp.int32)
    pair_starts = (pair_ends - pair_lengths).astype(jnp.int32)
    inside = (tile_index >= pair_starts) & (tile_index < pair_ends)
    first = jnp.sum(jnp.where(inside, pair_starts, 0)).astype(jnp.int32)
    count = jnp.sum(jnp.where(inside, pair_lengths, 0)).astype(jnp.int32)
    return first, count


def reference(queries, kv_cache, grad_out, pair_lengths):
    window = MOST * TILE
    softmax_scale = HD ** -0.5
    highest = lax.Precision.HIGHEST
    padded = jnp.concatenate([kv_cache, jnp.zeros((window, 2 * HD), kv_cache.dtype)], axis=0)

    def tile_step(grad_rows, tile_index):
        first, count = pair_span(pair_lengths, tile_index)
        start_row = (tile_index * TILE).astype(jnp.int32)
        query_tile = lax.dynamic_slice_in_dim(queries, start_row, TILE, 0).astype(jnp.float32).reshape(TILE, QH, HD)
        grad_tile = lax.dynamic_slice_in_dim(grad_out, start_row, TILE, 0).astype(jnp.float32).reshape(TILE, QH, HD)
        key_start = (first * TILE).astype(jnp.int32)
        nearby = lax.dynamic_slice_in_dim(padded, key_start, window, 0).astype(jnp.float32)
        key_block = nearby[:, :HD]
        value_block = nearby[:, HD:]
        inside = jnp.arange(window, dtype=jnp.int32) < count * TILE
        scores = jnp.einsum("rhc,kc->rhk", query_tile, key_block, precision=highest) * softmax_scale
        scores = jnp.where(inside[None, None, :], scores, -jnp.inf)
        log_total = jax.nn.logsumexp(scores, axis=2)
        attention = jnp.exp(scores - log_total[:, :, None])
        grad_probs = jnp.einsum("rhc,kc->rhk", grad_tile, value_block, precision=highest)
        row_delta = jnp.sum(attention * grad_probs, axis=2)
        attention_low = lax.optimization_barrier(attention.astype(jnp.bfloat16)).astype(jnp.float32)
        grad_scores = lax.optimization_barrier((attention * (grad_probs - row_delta[:, :, None])).astype(jnp.bfloat16)).astype(jnp.float32)
        grad_query = jnp.einsum("rhk,kc->rhc", grad_scores, key_block, precision=highest) * softmax_scale
        grad_query = grad_query.astype(jnp.bfloat16).reshape(TILE, QH * HD)
        grad_keys = jnp.einsum("rhk,rhc->kc", grad_scores, query_tile, precision=highest) * softmax_scale
        grad_values = jnp.einsum("rhk,rhc->kc", attention_low, grad_tile, precision=highest)
        previous = lax.dynamic_slice_in_dim(grad_rows, key_start, window, 0)
        grad_rows = lax.dynamic_update_slice_in_dim(grad_rows, previous + jnp.concatenate([grad_keys, grad_values], axis=1), key_start, 0)
        return grad_rows, grad_query

    start_rows = jnp.zeros((TOKENS + window, 2 * HD), jnp.float32)
    grad_rows, grad_tiles = lax.scan(tile_step, start_rows, jnp.arange(TILES_ALL, dtype=jnp.int32))
    return grad_tiles.reshape(TOKENS, QH * HD), grad_rows[:TOKENS]
```

```python
import functools

import jax
import jax.numpy as jnp
from jax import lax
from jax.experimental import pallas as pl
from jax.experimental.pallas import tpu as pltpu
from jax.sharding import PartitionSpec as P

HD = 128
QH = 8
HG = 4
TILE = 256
MOST = 12
STEP = 2
SCALE = HD**-0.5
SCALE_LOG2 = SCALE * 1.4426950408889634
F32 = jnp.float32
BF16 = jnp.bfloat16


def attention_kernel(
    reach, per_device, lengths, own_any, twin_any, q_ref, g_ref, dq_ref, own_out, twin_out,
    kv, acc, low, exps, gprobs, maxes, keys_t, q_t, g_t, dq_t, in_sems, out_sems,
):
    pieces = 2 * reach + 1
    rows_dev = per_device * TILE
    me = lax.axis_index("dp")
    core = lax.rem(me, 2)
    base_tile = (me // 2 - reach) * 2 * per_device

    def near(piece, which):
        return pl.ds(pl.multiple_of((piece * 2 + which) * rows_dev, rows_dev), rows_dev)

    def far(piece):
        return pl.ds(piece * rows_dev, rows_dev)

    loads = []
    for piece in range(pieces):
        for side, (source, which) in enumerate(((own_any, core), (twin_any, 1 - core))):
            loads.append(
                pltpu.make_async_copy(
                    source.at[far(piece)], kv.at[near(piece, which)], in_sems.at[side, piece]
                )
            )
    for load in loads:
        load.start()
    acc[...] = jnp.zeros_like(acc)
    for load in loads:
        load.wait()

    groups = QH // HG

    def unit(index, _):
        tile = index // groups
        group = index % groups
        own_tile = me * per_device + tile
        first = jnp.int32(0)
        count = jnp.int32(0)
        end = jnp.int32(0)
        for pair in range(lengths.shape[0]):
            start = end
            size = lengths[pair]
            end = start + size
            inside = (own_tile >= start) & (own_tile < end)
            first = jnp.where(inside, start, first)
            count = jnp.where(inside, size, count)
        first = first - base_tile
        rows = pl.ds(pl.multiple_of(tile * TILE, TILE), TILE)

        def cols(head):
            return pl.ds(pl.multiple_of((group * HG + head) * HD, HD), HD)

        def kv_rows(block, blocks):
            return pl.ds(pl.multiple_of((first + block) * TILE, TILE), blocks * TILE)

        def local(block, blocks):
            return pl.ds(pl.multiple_of(block * TILE, TILE), blocks * TILE)

        @pl.when(group == 0)
        def _():
            def turn(block, _):
                keys_t[:, local(block, 1)] = kv[kv_rows(block, 1), :HD].T
                return 0

            lax.fori_loop(0, count, turn, 0)

        for head in range(HG):
            q_t[head] = q_ref[rows, cols(head)].T
            g_t[head] = g_ref[rows, cols(head)].T

        def sweep(step, state):
            whole = count // STEP
            state = lax.fori_loop(0, whole, lambda i, s: step(i * STEP, STEP, s), state)
            return lax.fori_loop(whole * STEP, count, lambda b, s: step(b, 1, s), state)

        def scores(block, blocks, state):
            at, here = kv_rows(block, blocks), local(block, blocks)
            done = []
            for head in range(HG):
                top, total, weighted = state[head]
                score = jnp.dot(kv[at, :HD], q_t[head], preferred_element_type=F32)
                gprob = jnp.dot(kv[at, HD:], g_t[head], preferred_element_type=F32)
                new_top = jnp.maximum(top, jnp.max(score, axis=0, keepdims=True))
                gprobs[head, here] = gprob
                weight = jnp.exp2((score - new_top) * SCALE_LOG2)
                fade = jnp.exp2((top - new_top) * SCALE_LOG2)
                total = total * fade + jnp.sum(weight, axis=0, keepdims=True)
                weighted = weighted * fade + jnp.sum(weight * gprob, axis=0, keepdims=True)
                exps[head, here] = weight
                maxes[head, block] = new_top
                done.append((new_top, total, weighted))
            return tuple(done)

        zero = jnp.zeros((1, TILE), F32)
        state = sweep(scores, tuple((jnp.full((1, TILE), -jnp.inf, F32), zero, zero) for _ in range(HG)))
        stats = tuple((top, 1.0 / total, weighted / total) for top, total, weighted in state)
        dq_t[...] = jnp.zeros_like(dq_t)

        def grads(block, blocks, _):
            at, here = kv_rows(block, blocks), local(block, blocks)
            key_t = keys_t[:, here]
            for head in range(HG):
                top, inverse, delta = stats[head]
                factor = jnp.exp2((maxes[head, block] - top) * SCALE_LOG2) * inverse
                prob = exps[head, here] * factor
                dscore = (prob * (gprobs[head, here] - delta)).astype(BF16)
                prob = prob.astype(BF16)
                dq_t[head] += jnp.dot(key_t, dscore, preferred_element_type=F32)
                acc[at, :HD] += jnp.dot(dscore, q_ref[rows, cols(head)], preferred_element_type=F32) * SCALE
                acc[at, HD:] += jnp.dot(prob, g_ref[rows, cols(head)], preferred_element_type=F32)
            return 0

        sweep(grads, 0)
        for head in range(HG):
            dq_ref[rows, cols(head)] = (dq_t[head] * SCALE).T.astype(BF16)
        return 0

    lax.fori_loop(0, per_device * groups, unit, 0)

    stores = []
    for piece in range(pieces):
        stores.append(
            pltpu.make_async_copy(acc.at[near(piece, core)], own_out.at[far(piece)], out_sems.at[0, piece])
        )
        stores[-1].start()
    low[...] = acc[...].astype(BF16)
    for piece in range(pieces):
        stores.append(
            pltpu.make_async_copy(low.at[near(piece, 1 - core)], twin_out.at[far(piece)], out_sems.at[1, piece])
        )
        stores[-1].start()
    for store in stores:
        store.wait()


def attention(reach, lengths, own, twin, queries, grad_out):
    pieces = 2 * reach + 1
    rows_dev = queries.shape[0]
    per_device = rows_dev // TILE
    near_rows = 2 * pieces * rows_dev
    vmem = pl.BlockSpec(memory_space=pltpu.VMEM)
    hbm = pl.BlockSpec(memory_space=pl.ANY)
    return pl.pallas_call(
        functools.partial(attention_kernel, reach, per_device),
        out_shape=(
            jax.ShapeDtypeStruct(queries.shape, BF16),
            jax.ShapeDtypeStruct((pieces * rows_dev, 2 * HD), F32),
            jax.ShapeDtypeStruct((pieces * rows_dev, 2 * HD), BF16),
        ),
        in_specs=[pl.BlockSpec(memory_space=pltpu.SMEM), hbm, hbm, vmem, vmem],
        out_specs=(vmem, hbm, hbm),
        scratch_shapes=[
            pltpu.VMEM((near_rows, 2 * HD), BF16),
            pltpu.VMEM((near_rows, 2 * HD), F32),
            pltpu.VMEM((near_rows, 2 * HD), BF16),
            pltpu.VMEM((HG, MOST * TILE, TILE), F32),
            pltpu.VMEM((HG, MOST * TILE, TILE), F32),
            pltpu.VMEM((HG, MOST, 1, TILE), F32),
            pltpu.VMEM((HD, MOST * TILE), BF16),
            pltpu.VMEM((HG, HD, TILE), BF16),
            pltpu.VMEM((HG, HD, TILE), BF16),
            pltpu.VMEM((HG, HD, TILE), F32),
            pltpu.SemaphoreType.DMA((2, pieces)),
            pltpu.SemaphoreType.DMA((2, pieces)),
        ],
        compiler_params=pltpu.CompilerParams(vmem_limit_bytes=60 * 2**20),
    )(lengths, own, twin, queries, grad_out)


def body(queries, kv_cache, grad_out, pair_lengths):
    rows_dev = queries.shape[0]
    per_chip = 2 * rows_dev // TILE
    reach = (MOST - 1 + per_chip - 1) // per_chip
    count = lax.axis_size("dp")

    def by_chips(value, chips):
        steps = 2 * chips
        return lax.ppermute(
            value, "dp", [(i, i + steps) for i in range(count) if 0 <= i + steps < count]
        )

    def to_twin(value):
        return lax.ppermute(value, "dp", [(i, i ^ 1) for i in range(count)])

    own = jnp.concatenate(
        [kv_cache if chips == 0 else by_chips(kv_cache, -chips) for chips in range(-reach, reach + 1)], axis=0
    )
    twin = to_twin(own)
    grad_queries, own_grad, twin_grad = attention(reach, pair_lengths, own, twin, queries, grad_out)
    summed = own_grad + to_twin(twin_grad).astype(F32)
    grad_kv = summed[reach * rows_dev : (reach + 1) * rows_dev]
    for chips in range(-reach, reach + 1):
        if chips != 0:
            low = (chips + reach) * rows_dev
            grad_kv = grad_kv + by_chips(summed[low : low + rows_dev].astype(BF16), chips).astype(F32)
    return grad_queries, grad_kv


def solution(mesh):
    tokens = P(("groups", "dp"), None)
    return jax.shard_map(
        body,
        mesh=mesh,
        in_specs=(tokens, tokens, tokens, P("groups")),
        out_specs=(tokens, tokens),
        check_vma=False,
    )
```

```python
import functools

import jax
import jax.numpy as jnp
from jax import lax
from jax.experimental import pallas as pl
from jax.experimental.pallas import tpu as pltpu
from jax.sharding import PartitionSpec as P

HD = 128
QH = 8
HG = 4
TILE = 256
MOST = 12
STEP = 6
SCALE = HD**-0.5
SCALE_LOG2 = SCALE * 1.4426950408889634
F32 = jnp.float32
BF16 = jnp.bfloat16


RELATIONS = ("self", "row", "up", "down", "up_across", "down_across", "two_rows")


def chip_step(relation, column):
    return (0, 1 - 2 * column, 2, -2, 3 - 2 * column, -1 - 2 * column, 6 * column - 3)[relation]


def attention_kernel(
    reach, per_device, lengths, own_any, twin_any, q_ref, g_ref, dq_ref, own_out, twin_out,
    kv, acc, low, exps, gprobs, maxes, keys_t, q_t, g_t, dq_t, in_sems, out_sems,
):
    pieces = 2 * reach + 1
    rows_dev = per_device * TILE
    me = lax.axis_index("dp")
    core = lax.rem(me, 2)
    column = lax.rem(me // 2, 2)
    base_tile = (me // 2 - reach) * 2 * per_device

    def near(piece, which):
        place = reach + chip_step(piece, column)
        return pl.ds(pl.multiple_of((place * 2 + which) * rows_dev, rows_dev), rows_dev)

    def far(piece):
        return pl.ds(piece * rows_dev, rows_dev)

    loads = []
    for piece in range(pieces):
        for side, (source, which) in enumerate(((own_any, core), (twin_any, 1 - core))):
            loads.append(
                pltpu.make_async_copy(
                    source.at[far(piece)], kv.at[near(piece, which)], in_sems.at[side, piece]
                )
            )
    for load in loads:
        load.start()
    acc[...] = jnp.zeros_like(acc)
    for load in loads:
        load.wait()

    groups = QH // HG

    def unit(index, _):
        tile = index // groups
        group = index % groups
        own_tile = me * per_device + tile
        first = jnp.int32(0)
        count = jnp.int32(0)
        end = jnp.int32(0)
        for pair in range(lengths.shape[0]):
            start = end
            size = lengths[pair]
            end = start + size
            inside = (own_tile >= start) & (own_tile < end)
            first = jnp.where(inside, start, first)
            count = jnp.where(inside, size, count)
        first = first - base_tile
        rows = pl.ds(pl.multiple_of(tile * TILE, TILE), TILE)

        def cols(head):
            return pl.ds(pl.multiple_of((group * HG + head) * HD, HD), HD)

        def kv_rows(block, blocks):
            return pl.ds(pl.multiple_of((first + block) * TILE, TILE), blocks * TILE)

        def local(block, blocks):
            return pl.ds(pl.multiple_of(block * TILE, TILE), blocks * TILE)

        @pl.when(group == 0)
        def _():
            def turn(block, _):
                keys_t[:, local(block, 1)] = kv[kv_rows(block, 1), :HD].T
                return 0

            lax.fori_loop(0, count, turn, 0)

        for head in range(HG):
            q_t[head] = q_ref[rows, cols(head)].T
            g_t[head] = g_ref[rows, cols(head)].T

        def sweep(step, state):
            whole = count // STEP
            state = lax.fori_loop(0, whole, lambda i, s: step(i * STEP, STEP, s), state)
            return lax.fori_loop(whole * STEP, count, lambda b, s: step(b, 1, s), state)

        def scores(block, blocks, state):
            at, here = kv_rows(block, blocks), local(block, blocks)
            done = []
            for head in range(HG):
                top, total, weighted = state[head]
                score = jnp.dot(kv[at, :HD], q_t[head], preferred_element_type=F32)
                gprob = jnp.dot(kv[at, HD:], g_t[head], preferred_element_type=F32)
                new_top = jnp.maximum(top, jnp.max(score, axis=0, keepdims=True))
                gprobs[head, here] = gprob
                weight = jnp.exp2((score - new_top) * SCALE_LOG2)
                fade = jnp.exp2((top - new_top) * SCALE_LOG2)
                total = total * fade + jnp.sum(weight, axis=0, keepdims=True)
                weighted = weighted * fade + jnp.sum(weight * gprob, axis=0, keepdims=True)
                exps[head, here] = weight
                maxes[head, block] = new_top
                done.append((new_top, total, weighted))
            return tuple(done)

        zero = jnp.zeros((1, TILE), F32)
        state = sweep(scores, tuple((jnp.full((1, TILE), -jnp.inf, F32), zero, zero) for _ in range(HG)))
        stats = tuple((top, 1.0 / total, weighted / total) for top, total, weighted in state)
        dq_t[...] = jnp.zeros_like(dq_t)

        def grads(block, blocks, _):
            at, here = kv_rows(block, blocks), local(block, blocks)
            key_t = keys_t[:, here]
            for head in range(HG):
                top, inverse, delta = stats[head]
                factor = jnp.exp2((maxes[head, block] - top) * SCALE_LOG2) * inverse
                prob = exps[head, here] * factor
                dscore = (prob * (gprobs[head, here] - delta)).astype(BF16)
                prob = prob.astype(BF16)
                dq_t[head] += jnp.dot(key_t, dscore, preferred_element_type=F32)
                acc[at, :HD] += jnp.dot(dscore, q_ref[rows, cols(head)], preferred_element_type=F32) * SCALE
                acc[at, HD:] += jnp.dot(prob, g_ref[rows, cols(head)], preferred_element_type=F32)
            return 0

        sweep(grads, 0)
        for head in range(HG):
            dq_ref[rows, cols(head)] = (dq_t[head] * SCALE).T.astype(BF16)
        return 0

    lax.fori_loop(0, per_device * groups, unit, 0)

    stores = []
    for piece in range(pieces):
        stores.append(
            pltpu.make_async_copy(acc.at[near(piece, core)], own_out.at[far(piece)], out_sems.at[0, piece])
        )
        stores[-1].start()
    low[...] = acc[...].astype(BF16)
    for piece in range(pieces):
        stores.append(
            pltpu.make_async_copy(low.at[near(piece, 1 - core)], twin_out.at[far(piece)], out_sems.at[1, piece])
        )
        stores[-1].start()
    for store in stores:
        store.wait()


def attention(reach, lengths, own, twin, queries, grad_out):
    pieces = 2 * reach + 1
    rows_dev = queries.shape[0]
    per_device = rows_dev // TILE
    near_rows = 2 * pieces * rows_dev
    vmem = pl.BlockSpec(memory_space=pltpu.VMEM)
    hbm = pl.BlockSpec(memory_space=pl.ANY)
    return pl.pallas_call(
        functools.partial(attention_kernel, reach, per_device),
        out_shape=(
            jax.ShapeDtypeStruct(queries.shape, BF16),
            jax.ShapeDtypeStruct((pieces * rows_dev, 2 * HD), F32),
            jax.ShapeDtypeStruct((pieces * rows_dev, 2 * HD), BF16),
        ),
        in_specs=[pl.BlockSpec(memory_space=pltpu.SMEM), hbm, hbm, vmem, vmem],
        out_specs=(vmem, hbm, hbm),
        scratch_shapes=[
            pltpu.VMEM((near_rows, 2 * HD), BF16),
            pltpu.VMEM((near_rows, 2 * HD), F32),
            pltpu.VMEM((near_rows, 2 * HD), BF16),
            pltpu.VMEM((HG, MOST * TILE, TILE), F32),
            pltpu.VMEM((HG, MOST * TILE, TILE), F32),
            pltpu.VMEM((HG, MOST, 1, TILE), F32),
            pltpu.VMEM((HD, MOST * TILE), BF16),
            pltpu.VMEM((HG, HD, TILE), BF16),
            pltpu.VMEM((HG, HD, TILE), BF16),
            pltpu.VMEM((HG, HD, TILE), F32),
            pltpu.SemaphoreType.DMA((2, pieces)),
            pltpu.SemaphoreType.DMA((2, pieces)),
        ],
        compiler_params=pltpu.CompilerParams(vmem_limit_bytes=60 * 2**20),
    )(lengths, own, twin, queries, grad_out)


def body(queries, kv_cache, grad_out, pair_lengths):
    rows_dev = queries.shape[0]
    reach = 3
    assert 2 * rows_dev * reach >= (MOST - 1) * TILE
    count = lax.axis_size("dp")

    def send(value, relation, back):
        pairs = []
        for source in range(count):
            row, column, core = source // 4, (source // 2) % 2, source % 2
            rows, across = {
                "row": (0, 1),
                "up": (1, 0),
                "down": (-1, 0),
                "up_across": (1, 1),
                "down_across": (-1, 1),
                "two_rows": (4 * column - 2, 1),
            }[relation]
            if back and relation != "two_rows":
                rows = -rows
            if 0 <= row + rows < count // 4:
                pairs.append((source, (row + rows) * 4 + (column ^ across) * 2 + core))
        return lax.ppermute(value, "dp", pairs)

    def to_twin(value):
        return lax.ppermute(value, "dp", [(i, i ^ 1) for i in range(count)])

    own = jnp.concatenate(
        [kv_cache] + [send(kv_cache, relation, True) for relation in RELATIONS[1:]], axis=0
    )
    twin = to_twin(own)
    grad_queries, own_grad, twin_grad = attention(reach, pair_lengths, own, twin, queries, grad_out)
    summed = own_grad + to_twin(twin_grad).astype(F32)
    grad_kv = summed[:rows_dev]
    for piece, relation in enumerate(RELATIONS[1:], 1):
        share = summed[piece * rows_dev : (piece + 1) * rows_dev].astype(BF16)
        grad_kv = grad_kv + send(share, relation, False).astype(F32)
    return grad_queries, grad_kv


def solution(mesh):
    tokens = P(("groups", "dp"), None)
    return jax.shard_map(
        body,
        mesh=mesh,
        in_specs=(tokens, tokens, tokens, P("groups")),
        out_specs=(tokens, tokens),
        check_vma=False,
    )
```

```python
import functools

import jax
import jax.numpy as jnp
from jax import lax
from jax.experimental import pallas as pl
from jax.experimental.pallas import tpu as pltpu
from jax.sharding import PartitionSpec as P

HD = 128
QH = 8
HG = 4
TILE = 256
MOST = 12
STEP = 4
REACH = 3
SCALE = HD**-0.5
SCALE_LOG2 = SCALE * 1.4426950408889634
F32 = jnp.float32
BF16 = jnp.bfloat16
GROUPS = QH // HG

ROUNDS = (("row", "two_rows"), ("up_across", "down_across"), ("up", "down"))


def chip_step(relation, column):
    return {
        "row": 1 - 2 * column,
        "up": 2,
        "down": -2,
        "up_across": 3 - 2 * column,
        "down_across": -1 - 2 * column,
        "two_rows": 6 * column - 3,
    }[relation]


class Place:
    def __init__(self, lengths, per_device, index):
        me = lax.axis_index("dp")
        per_chip = 2 * per_device
        tile = index // GROUPS
        self.group = index % GROUPS
        own_tile = me * per_device + tile
        first = jnp.int32(0)
        last = jnp.int32(0)
        end = jnp.int32(0)
        for pair in range(lengths.shape[0]):
            start = end
            end = start + lengths[pair]
            inside = (own_tile >= start) & (own_tile < end)
            first = jnp.where(inside, start, first)
            last = jnp.where(inside, end, last)
        chip_start = (me // 2) * per_chip
        chip_end = chip_start + per_chip
        below = jnp.maximum(chip_start - first, 0)
        above = jnp.maximum(last - chip_end, 0)
        self.far_base = REACH * per_chip - below
        self.far_count = below + above
        self.own_base = jnp.maximum(first, chip_start) - chip_start
        self.own_count = jnp.minimum(last, chip_end) - chip_start - self.own_base
        self.rows = pl.ds(pl.multiple_of(tile * TILE, TILE), TILE)
        self.slot = tile * QH + self.group * HG

    def cols(self, head):
        return pl.ds(pl.multiple_of((self.group * HG + head) * HD, HD), HD)


def tiles(block, blocks):
    return pl.ds(pl.multiple_of(block * TILE, TILE), blocks * TILE)


def sweep(count, step, state):
    whole = count // STEP
    state = lax.fori_loop(0, whole, lambda i, s: step(i * STEP, STEP, s), state)
    return lax.fori_loop(whole * STEP, count, lambda b, s: step(b, 1, s), state)


def products(place, kv, at, q_t, g_t, head):
    score = jnp.dot(kv[at, :HD], q_t[head], preferred_element_type=F32)
    gprob = jnp.dot(kv[at, HD:], g_t[head], preferred_element_type=F32)
    return score, gprob


def gathered(state, score, gprob):
    top, total, weighted = state
    new_top = jnp.maximum(top, jnp.max(score, axis=0, keepdims=True))
    weight = jnp.exp2((score - new_top) * SCALE_LOG2)
    fade = jnp.exp2((top - new_top) * SCALE_LOG2)
    total = total * fade + jnp.sum(weight, axis=0, keepdims=True)
    weighted = weighted * fade + jnp.sum(weight * gprob, axis=0, keepdims=True)
    return (new_top, total, weighted), weight


def turn_rows(place, q_ref, g_ref, q_t, g_t):
    for head in range(HG):
        q_t[head] = q_ref[place.rows, place.cols(head)].T
        g_t[head] = g_ref[place.rows, place.cols(head)].T


def load_chip(chip_any, kv, sems, rows_dev, core):
    copies = []
    for half, which in enumerate((core, 1 - core)):
        to = pl.ds(pl.multiple_of(which * rows_dev, rows_dev), rows_dev)
        copies.append(
            pltpu.make_async_copy(chip_any.at[pl.ds(half * rows_dev, rows_dev)], kv.at[to], sems.at[half])
        )
        copies[-1].start()
    return copies


def own_stats_kernel(per_device, lengths, chip_any, q_ref, g_ref, stats_ref, kv, q_t, g_t, sems):
    core = lax.rem(lax.axis_index("dp"), 2)
    for copy in load_chip(chip_any, kv, sems, per_device * TILE, core):
        copy.wait()

    def unit(index, _):
        place = Place(lengths, per_device, index)
        turn_rows(place, q_ref, g_ref, q_t, g_t)

        def step(block, blocks, state):
            at = tiles(place.own_base + block, blocks)
            return tuple(
                gathered(state[head], *products(place, kv, at, q_t, g_t, head))[0] for head in range(HG)
            )

        zero = jnp.zeros((1, TILE), F32)
        start = tuple((jnp.full((1, TILE), -jnp.inf, F32), zero, zero) for _ in range(HG))
        state = sweep(place.own_count, step, start)
        for head in range(HG):
            for row in range(3):
                stats_ref[place.slot + head, row : row + 1] = state[head][row]
        return 0

    lax.fori_loop(0, per_device * GROUPS, unit, 0)


def far_kernel(
    per_device, lengths, mine_any, twin_any, q_ref, g_ref, stats_in, dq_ref, stats_ref, mine_out, twin_out,
    kv, acc, low, exps, gprobs, maxes, keys_t, q_t, g_t, in_sems, out_sems,
):
    rows_dev = per_device * TILE
    me = lax.axis_index("dp")
    core = lax.rem(me, 2)
    column = lax.rem(me // 2, 2)

    def near(number, carrier, which):
        steps = [chip_step(relation, column) for relation in ROUNDS[number]]
        step = jnp.where(carrier == 0, steps[0], steps[1])
        chip = jnp.where(step < 0, step + REACH, step + REACH - 1)
        return pl.ds(pl.multiple_of((chip * 2 + which) * rows_dev, rows_dev), rows_dev)

    def halves():
        for number in range(len(ROUNDS)):
            for half in range(2):
                at = pl.ds((number * 2 + half) * rows_dev, rows_dev)
                yield number, half, at

    loads = []
    for number, half, at in halves():
        for side, (source, carrier) in enumerate(((mine_any, core), (twin_any, 1 - core))):
            which = carrier if half == 0 else 1 - carrier
            loads.append(
                pltpu.make_async_copy(
                    source.at[at], kv.at[near(number, carrier, which)], in_sems.at[side, number, half]
                )
            )
            loads[-1].start()
    acc[...] = jnp.zeros_like(acc)
    for load in loads:
        load.wait()

    def unit(index, _):
        place = Place(lengths, per_device, index)

        @pl.when(place.group == 0)
        def _():
            def turn(block, _):
                keys_t[:, tiles(block, 1)] = kv[tiles(place.far_base + block, 1), :HD].T
                return 0

            lax.fori_loop(0, place.far_count, turn, 0)

        turn_rows(place, q_ref, g_ref, q_t, g_t)

        def scores(block, blocks, state):
            at, here = tiles(place.far_base + block, blocks), tiles(block, blocks)
            done = []
            for head in range(HG):
                score, gprob = products(place, kv, at, q_t, g_t, head)
                gprobs[head, here] = gprob
                after, weight = gathered(state[head], score, gprob)
                exps[head, here] = weight
                maxes[head, block] = after[0]
                done.append(after)
            return tuple(done)

        start = tuple(
            tuple(stats_in[place.slot + head, row : row + 1] for row in range(3)) for head in range(HG)
        )
        state = sweep(place.far_count, scores, start)
        stats = tuple((top, 1.0 / total, weighted / total) for top, total, weighted in state)
        for head in range(HG):
            top, total, weighted = state[head]
            stats_ref[place.slot + head, 0:1] = top * SCALE_LOG2 + jnp.log2(total)
            stats_ref[place.slot + head, 1:2] = weighted / total
            dq_ref[place.slot + head] = jnp.zeros((HD, TILE), F32)

        def grads(block, blocks, _):
            at, here = tiles(place.far_base + block, blocks), tiles(block, blocks)
            key_t = keys_t[:, here]
            for head in range(HG):
                top, inverse, delta = stats[head]
                factor = jnp.exp2((maxes[head, block] - top) * SCALE_LOG2) * inverse
                prob = exps[head, here] * factor
                dscore = (prob * (gprobs[head, here] - delta)).astype(BF16)
                prob = prob.astype(BF16)
                dq_ref[place.slot + head] += jnp.dot(key_t, dscore, preferred_element_type=F32)
                acc[at, :HD] += SCALE * jnp.dot(
                    dscore, q_ref[place.rows, place.cols(head)], preferred_element_type=F32
                )
                acc[at, HD:] += jnp.dot(prob, g_ref[place.rows, place.cols(head)], preferred_element_type=F32)
            return 0

        sweep(place.far_count, grads, 0)
        return 0

    lax.fori_loop(0, per_device * GROUPS, unit, 0)

    low[...] = acc[...].astype(BF16)
    stores = []
    for number, half, at in halves():
        for side, (source, out, carrier) in enumerate(((acc, mine_out, core), (low, twin_out, 1 - core))):
            which = carrier if half == 0 else 1 - carrier
            stores.append(
                pltpu.make_async_copy(
                    source.at[near(number, carrier, which)], out.at[at], out_sems.at[side, number, half]
                )
            )
            stores[-1].start()
    for store in stores:
        store.wait()


def own_grads_kernel(
    per_device, lengths, chip_any, q_ref, g_ref, stats_ref, dq_in, dq_ref, own_out,
    kv, acc, keys_t, q_t, g_t, dq_t, sems, out_sems,
):
    rows_dev = per_device * TILE
    core = lax.rem(lax.axis_index("dp"), 2)
    loads = load_chip(chip_any, kv, sems, rows_dev, core)
    acc[...] = jnp.zeros_like(acc)
    for load in loads:
        load.wait()
    for block in range(2 * per_device):
        keys_t[block] = kv[block * TILE : (block + 1) * TILE, :HD].T

    def unit(index, _):
        place = Place(lengths, per_device, index)
        turn_rows(place, q_ref, g_ref, q_t, g_t)
        for head in range(HG):
            dq_t[head] = dq_in[place.slot + head]

        def grads(block, blocks, _):
            at = tiles(place.own_base + block, blocks)
            for head in range(HG):
                score, gprob = products(place, kv, at, q_t, g_t, head)
                prob = jnp.exp2(score * SCALE_LOG2 - stats_ref[place.slot + head, 0:1])
                dscore = (prob * (gprob - stats_ref[place.slot + head, 1:2])).astype(BF16)
                prob = prob.astype(BF16)
                dq = dq_t[head]
                for turn in range(blocks):
                    dq = dq + jnp.dot(
                        keys_t[place.own_base + block + turn],
                        dscore[turn * TILE : (turn + 1) * TILE],
                        preferred_element_type=F32,
                    )
                dq_t[head] = dq
                acc[at, :HD] += SCALE * jnp.dot(
                    dscore, q_ref[place.rows, place.cols(head)], preferred_element_type=F32
                )
                acc[at, HD:] += jnp.dot(prob, g_ref[place.rows, place.cols(head)], preferred_element_type=F32)
            return 0

        sweep(place.own_count, grads, 0)
        for head in range(HG):
            dq_ref[place.rows, place.cols(head)] = (dq_t[head] * SCALE).T.astype(BF16)
        return 0

    lax.fori_loop(0, per_device * GROUPS, unit, 0)
    stores = []
    for half, which in enumerate((core, 1 - core)):
        source = pl.ds(pl.multiple_of(which * rows_dev, rows_dev), rows_dev)
        stores.append(
            pltpu.make_async_copy(acc.at[source], own_out.at[pl.ds(half * rows_dev, rows_dev)], out_sems.at[half])
        )
        stores[-1].start()
    for store in stores:
        store.wait()


def body(queries, kv_cache, grad_out, pair_lengths):
    rows_dev = queries.shape[0]
    per_device = rows_dev // TILE
    assert 2 * per_device * REACH >= MOST - 1
    count = lax.axis_size("dp")
    chip_rows = 2 * rows_dev
    far_rows = 2 * REACH * chip_rows
    mine_rows = REACH * chip_rows
    slots = per_device * QH

    def send(value, number, back):
        pairs = []
        for source in range(count):
            row, column, core = source // 4, (source // 2) % 2, source % 2
            relation = ROUNDS[number][core]
            rows, across = {
                "row": (0, 1),
                "up": (1, 0),
                "down": (-1, 0),
                "up_across": (1, 1),
                "down_across": (-1, 1),
                "two_rows": (4 * column - 2, 1),
            }[relation]
            if back and relation != "two_rows":
                rows = -rows
            if 0 <= row + rows < count // 4:
                pairs.append((source, (row + rows) * 4 + (column ^ across) * 2 + core))
        return lax.ppermute(value, "dp", pairs)

    def to_twin(value):
        return lax.ppermute(value, "dp", [(i, i ^ 1) for i in range(count)])

    vmem = pl.BlockSpec(memory_space=pltpu.VMEM)
    hbm = pl.BlockSpec(memory_space=pl.ANY)
    smem = pl.BlockSpec(memory_space=pltpu.SMEM)
    turned = pltpu.VMEM((HG, HD, TILE), BF16)
    stats_shape = jax.ShapeDtypeStruct((slots, 8, TILE), F32)
    product = 2 * QH * TILE * TILE * HD * per_device

    def cost(products_done):
        return pl.CostEstimate(flops=3 * products_done * product, bytes_accessed=2**23, transcendentals=0)

    chip = jnp.concatenate([kv_cache, to_twin(kv_cache)], axis=0)
    arrived = [send(chip, number, True) for number in range(len(ROUNDS))]
    own_stats = pl.pallas_call(
        functools.partial(own_stats_kernel, per_device),
        out_shape=stats_shape,
        in_specs=[smem, hbm, vmem, vmem],
        out_specs=vmem,
        scratch_shapes=[pltpu.VMEM((chip_rows, 2 * HD), BF16), turned, turned, pltpu.SemaphoreType.DMA((2,))],
        compiler_params=pltpu.CompilerParams(vmem_limit_bytes=24 * 2**20),
        cost_estimate=cost(8),
        name="own_stats",
    )(pair_lengths, chip, queries, grad_out)

    arrived, own_stats = lax.optimization_barrier((arrived, own_stats))
    mine = jnp.concatenate(arrived, axis=0)
    dq_far, stats, mine_grad, twin_grad = pl.pallas_call(
        functools.partial(far_kernel, per_device),
        out_shape=(
            jax.ShapeDtypeStruct((slots, HD, TILE), F32),
            stats_shape,
            jax.ShapeDtypeStruct((mine_rows, 2 * HD), F32),
            jax.ShapeDtypeStruct((mine_rows, 2 * HD), BF16),
        ),
        in_specs=[smem, hbm, hbm, vmem, vmem, vmem],
        out_specs=(vmem, vmem, hbm, hbm),
        scratch_shapes=[
            pltpu.VMEM((far_rows, 2 * HD), BF16),
            pltpu.VMEM((far_rows, 2 * HD), F32),
            pltpu.VMEM((far_rows, 2 * HD), BF16),
            pltpu.VMEM((HG, MOST * TILE, TILE), F32),
            pltpu.VMEM((HG, MOST * TILE, TILE), F32),
            pltpu.VMEM((HG, MOST, 1, TILE), F32),
            pltpu.VMEM((HD, MOST * TILE), BF16),
            turned,
            turned,
            pltpu.SemaphoreType.DMA((2, len(ROUNDS), 2)),
            pltpu.SemaphoreType.DMA((2, len(ROUNDS), 2)),
        ],
        compiler_params=pltpu.CompilerParams(vmem_limit_bytes=60 * 2**20),
        cost_estimate=cost(40),
        name="far",
    )(pair_lengths, mine, to_twin(mine), queries, grad_out, own_stats)

    leaving = (mine_grad + to_twin(twin_grad).astype(F32)).astype(BF16)
    landed = [
        send(leaving[number * chip_rows : (number + 1) * chip_rows], number, False)
        for number in range(len(ROUNDS))
    ]
    grad_queries, own_grad = pl.pallas_call(
        functools.partial(own_grads_kernel, per_device),
        out_shape=(
            jax.ShapeDtypeStruct(queries.shape, BF16),
            jax.ShapeDtypeStruct((chip_rows, 2 * HD), F32),
        ),
        in_specs=[smem, hbm, vmem, vmem, vmem, vmem],
        out_specs=(vmem, hbm),
        scratch_shapes=[
            pltpu.VMEM((chip_rows, 2 * HD), BF16),
            pltpu.VMEM((chip_rows, 2 * HD), F32),
            pltpu.VMEM((2 * per_device, HD, TILE), BF16),
            turned,
            turned,
            pltpu.VMEM((HG, HD, TILE), F32),
            pltpu.SemaphoreType.DMA((2,)),
            pltpu.SemaphoreType.DMA((2,)),
        ],
        compiler_params=pltpu.CompilerParams(vmem_limit_bytes=32 * 2**20),
        cost_estimate=cost(20),
        name="own_grads",
    )(pair_lengths, chip, queries, grad_out, stats, dq_far)
    total = own_grad
    for part in landed:
        total = total + part.astype(F32)
    grad_kv = total[:rows_dev] + to_twin(total[rows_dev:].astype(BF16)).astype(F32)
    return grad_queries, grad_kv


def solution(mesh):
    tokens = P(("groups", "dp"), None)
    return jax.shard_map(
        body,
        mesh=mesh,
        in_specs=(tokens, tokens, tokens, P("groups")),
        out_specs=(tokens, tokens),
        check_vma=False,
    )
```

```python
import functools

import jax
import jax.numpy as jnp
from jax import lax
from jax.experimental import pallas as pl
from jax.experimental.pallas import tpu as pltpu
from jax.sharding import PartitionSpec as P

HD = 128
QH = 8
HG = 4
TILE = 256
MOST = 12
FAR_STEPS = (8, 2, 1)
OWN_STEPS = (4, 2, 1)
REACH = 3
SCALE = HD**-0.5
SCALE_LOG2 = SCALE * 1.4426950408889634
F32 = jnp.float32
BF16 = jnp.bfloat16
GROUPS = QH // HG

ROUNDS = (("row", "two_rows"), ("up_across", "down_across"), ("up", "down"))


def chip_step(relation, column):
    return {
        "row": 1 - 2 * column,
        "up": 2,
        "down": -2,
        "up_across": 3 - 2 * column,
        "down_across": -1 - 2 * column,
        "two_rows": 6 * column - 3,
    }[relation]


class Place:
    def __init__(self, lengths, per_device, index):
        me = lax.axis_index("dp")
        per_chip = 2 * per_device
        tile = index // GROUPS
        self.group = index % GROUPS
        own_tile = me * per_device + tile
        first = jnp.int32(0)
        last = jnp.int32(0)
        end = jnp.int32(0)
        for pair in range(lengths.shape[0]):
            start = end
            end = start + lengths[pair]
            inside = (own_tile >= start) & (own_tile < end)
            first = jnp.where(inside, start, first)
            last = jnp.where(inside, end, last)
        chip_start = (me // 2) * per_chip
        chip_end = chip_start + per_chip
        below = jnp.maximum(chip_start - first, 0)
        above = jnp.maximum(last - chip_end, 0)
        self.far_base = REACH * per_chip - below
        self.far_count = below + above
        self.own_base = jnp.maximum(first, chip_start) - chip_start
        self.own_count = jnp.minimum(last, chip_end) - chip_start - self.own_base
        self.rows = pl.ds(pl.multiple_of(tile * TILE, TILE), TILE)
        self.slot = tile * QH + self.group * HG

    def cols(self, head):
        return pl.ds(pl.multiple_of((self.group * HG + head) * HD, HD), HD)


def tiles(block, blocks):
    return pl.ds(pl.multiple_of(block * TILE, TILE), blocks * TILE)


def sweep(count, sizes, step, state):
    done = 0
    for size in sizes:
        rounds = (count - done) // size
        state = lax.fori_loop(0, rounds, lambda i, s, d=done, n=size: step(d + i * n, n, s), state)
        done = done + rounds * size
    return state


def products(place, kv, at, q_t, g_t, head):
    score = jnp.dot(kv[at, :HD], q_t[head], preferred_element_type=F32)
    gprob = jnp.dot(kv[at, HD:], g_t[head], preferred_element_type=F32)
    return score, gprob


def gathered(state, score, gprob):
    top, total, weighted = state
    new_top = jnp.maximum(top, jnp.max(score, axis=0, keepdims=True))
    weight = jnp.exp2((score - new_top) * SCALE_LOG2)
    fade = jnp.exp2((top - new_top) * SCALE_LOG2)
    total = total * fade + jnp.sum(weight, axis=0, keepdims=True)
    weighted = weighted * fade + jnp.sum(weight * gprob, axis=0, keepdims=True)
    return (new_top, total, weighted), weight


def turn_rows(place, q_ref, g_ref, q_t, g_t):
    for head in range(HG):
        q_t[head] = q_ref[place.rows, place.cols(head)].T
        g_t[head] = g_ref[place.rows, place.cols(head)].T


def load_chip(chip_any, kv, sems, rows_dev, core):
    copies = []
    for half, which in enumerate((core, 1 - core)):
        to = pl.ds(pl.multiple_of(which * rows_dev, rows_dev), rows_dev)
        copies.append(
            pltpu.make_async_copy(chip_any.at[pl.ds(half * rows_dev, rows_dev)], kv.at[to], sems.at[half])
        )
        copies[-1].start()
    return copies


def own_stats_kernel(per_device, lengths, chip_any, q_ref, g_ref, stats_ref, kv, q_t, g_t, sems):
    core = lax.rem(lax.axis_index("dp"), 2)
    for copy in load_chip(chip_any, kv, sems, per_device * TILE, core):
        copy.wait()

    def unit(index, _):
        place = Place(lengths, per_device, index)
        turn_rows(place, q_ref, g_ref, q_t, g_t)

        def step(block, blocks, state):
            at = tiles(place.own_base + block, blocks)
            return tuple(
                gathered(state[head], *products(place, kv, at, q_t, g_t, head))[0] for head in range(HG)
            )

        zero = jnp.zeros((1, TILE), F32)
        start = tuple((jnp.full((1, TILE), -jnp.inf, F32), zero, zero) for _ in range(HG))
        state = sweep(place.own_count, OWN_STEPS, step, start)
        for head in range(HG):
            for row in range(3):
                stats_ref[place.slot + head, row : row + 1] = state[head][row]
        return 0

    lax.fori_loop(0, per_device * GROUPS, unit, 0)


def far_kernel(
    per_device, lengths, mine_0, mine_1, mine_2, twin_0, twin_1, twin_2, q_ref, g_ref, stats_in,
    dq_ref, stats_ref, mine_out_0, mine_out_1, mine_out_2, twin_out_0, twin_out_1, twin_out_2, kv, acc, low, exps, gprobs, maxes, keys_t, q_t, g_t, in_sems, out_sems,
):
    rows_dev = per_device * TILE
    me = lax.axis_index("dp")
    core = lax.rem(me, 2)
    column = lax.rem(me // 2, 2)

    def near(number, carrier, which):
        steps = [chip_step(relation, column) for relation in ROUNDS[number]]
        step = jnp.where(carrier == 0, steps[0], steps[1])
        chip = jnp.where(step < 0, step + REACH, step + REACH - 1)
        return pl.ds(pl.multiple_of((chip * 2 + which) * rows_dev, rows_dev), rows_dev)

    def halves():
        for number in range(len(ROUNDS)):
            for half in range(2):
                at = pl.ds(half * rows_dev, rows_dev)
                yield number, half, at

    arrived = ((mine_0, mine_1, mine_2), (twin_0, twin_1, twin_2))
    leaving = ((mine_out_0, mine_out_1, mine_out_2), (twin_out_0, twin_out_1, twin_out_2))
    loads = []
    for number, half, at in halves():
        for side, carrier in enumerate((core, 1 - core)):
            source = arrived[side][number]
            which = carrier if half == 0 else 1 - carrier
            loads.append(
                pltpu.make_async_copy(
                    source.at[at], kv.at[near(number, carrier, which)], in_sems.at[side, number, half]
                )
            )
            loads[-1].start()
    acc[...] = jnp.zeros_like(acc)
    for load in loads:
        load.wait()

    def unit(index, _):
        place = Place(lengths, per_device, index)

        @pl.when(place.group == 0)
        def _():
            def turn(block, _):
                keys_t[:, tiles(block, 1)] = kv[tiles(place.far_base + block, 1), :HD].T
                return 0

            lax.fori_loop(0, place.far_count, turn, 0)

        turn_rows(place, q_ref, g_ref, q_t, g_t)

        def scores(block, blocks, state):
            at, here = tiles(place.far_base + block, blocks), tiles(block, blocks)
            done = []
            for head in range(HG):
                score, gprob = products(place, kv, at, q_t, g_t, head)
                gprobs[head, here] = gprob
                after, weight = gathered(state[head], score, gprob)
                exps[head, here] = weight
                maxes[head, block] = after[0]
                done.append(after)
            return tuple(done)

        start = tuple(
            tuple(stats_in[place.slot + head, row : row + 1] for row in range(3)) for head in range(HG)
        )
        state = sweep(place.far_count, FAR_STEPS, scores, start)
        stats = tuple((top, 1.0 / total, weighted / total) for top, total, weighted in state)
        for head in range(HG):
            top, total, weighted = state[head]
            stats_ref[place.slot + head, 0:1] = top * SCALE_LOG2 + jnp.log2(total)
            stats_ref[place.slot + head, 1:2] = weighted / total
            dq_ref[place.slot + head] = jnp.zeros((HD, TILE), F32)

        def grads(block, blocks, _):
            at, here = tiles(place.far_base + block, blocks), tiles(block, blocks)
            key_t = keys_t[:, here]
            for head in range(HG):
                top, inverse, delta = stats[head]
                factor = jnp.exp2((maxes[head, block] - top) * SCALE_LOG2) * inverse
                prob = exps[head, here] * factor
                dscore = (prob * (gprobs[head, here] - delta)).astype(BF16)
                prob = prob.astype(BF16)
                dq_ref[place.slot + head] += jnp.dot(key_t, dscore, preferred_element_type=F32)
                acc[at, :HD] += SCALE * jnp.dot(
                    dscore, q_ref[place.rows, place.cols(head)], preferred_element_type=F32
                )
                acc[at, HD:] += jnp.dot(prob, g_ref[place.rows, place.cols(head)], preferred_element_type=F32)
            return 0

        sweep(place.far_count, FAR_STEPS, grads, 0)
        return 0

    lax.fori_loop(0, per_device * GROUPS, unit, 0)

    low[...] = acc[...].astype(BF16)
    stores = []
    for number, half, at in halves():
        for side, carrier in enumerate((core, 1 - core)):
            out = leaving[side][number]
            which = carrier if half == 0 else 1 - carrier
            stores.append(
                pltpu.make_async_copy(
                    low.at[near(number, carrier, which)], out.at[at], out_sems.at[side, number, half]
                )
            )
            stores[-1].start()
    for store in stores:
        store.wait()


def own_grads_kernel(
    per_device, lengths, chip_any, q_ref, g_ref, stats_ref, dq_in, dq_ref, own_out,
    kv, acc, keys_t, q_t, g_t, dq_t, sems, out_sems,
):
    rows_dev = per_device * TILE
    core = lax.rem(lax.axis_index("dp"), 2)
    loads = load_chip(chip_any, kv, sems, rows_dev, core)
    acc[...] = jnp.zeros_like(acc)
    for load in loads:
        load.wait()
    for block in range(2 * per_device):
        keys_t[block] = kv[block * TILE : (block + 1) * TILE, :HD].T

    def unit(index, _):
        place = Place(lengths, per_device, index)
        turn_rows(place, q_ref, g_ref, q_t, g_t)
        for head in range(HG):
            dq_t[head] = dq_in[place.slot + head]

        def grads(block, blocks, _):
            at = tiles(place.own_base + block, blocks)
            for head in range(HG):
                score, gprob = products(place, kv, at, q_t, g_t, head)
                prob = jnp.exp2(score * SCALE_LOG2 - stats_ref[place.slot + head, 0:1])
                dscore = (prob * (gprob - stats_ref[place.slot + head, 1:2])).astype(BF16)
                prob = prob.astype(BF16)
                dq = dq_t[head]
                for turn in range(blocks):
                    dq = dq + jnp.dot(
                        keys_t[place.own_base + block + turn],
                        dscore[turn * TILE : (turn + 1) * TILE],
                        preferred_element_type=F32,
                    )
                dq_t[head] = dq
                acc[at, :HD] += SCALE * jnp.dot(
                    dscore, q_ref[place.rows, place.cols(head)], preferred_element_type=F32
                )
                acc[at, HD:] += jnp.dot(prob, g_ref[place.rows, place.cols(head)], preferred_element_type=F32)
            return 0

        sweep(place.own_count, OWN_STEPS, grads, 0)
        for head in range(HG):
            dq_ref[place.rows, place.cols(head)] = (dq_t[head] * SCALE).T.astype(BF16)
        return 0

    lax.fori_loop(0, per_device * GROUPS, unit, 0)
    stores = []
    for half, which in enumerate((core, 1 - core)):
        source = pl.ds(pl.multiple_of(which * rows_dev, rows_dev), rows_dev)
        stores.append(
            pltpu.make_async_copy(acc.at[source], own_out.at[pl.ds(half * rows_dev, rows_dev)], out_sems.at[half])
        )
        stores[-1].start()
    for store in stores:
        store.wait()


def body(queries, kv_cache, grad_out, pair_lengths):
    rows_dev = queries.shape[0]
    per_device = rows_dev // TILE
    assert 2 * per_device * REACH >= MOST - 1
    count = lax.axis_size("dp")
    chip_rows = 2 * rows_dev
    far_rows = 2 * REACH * chip_rows
    slots = per_device * QH

    def send(value, number, back):
        pairs = []
        for source in range(count):
            row, column, core = source // 4, (source // 2) % 2, source % 2
            relation = ROUNDS[number][core]
            rows, across = {
                "row": (0, 1),
                "up": (1, 0),
                "down": (-1, 0),
                "up_across": (1, 1),
                "down_across": (-1, 1),
                "two_rows": (4 * column - 2, 1),
            }[relation]
            if back and relation != "two_rows":
                rows = -rows
            if 0 <= row + rows < count // 4:
                pairs.append((source, (row + rows) * 4 + (column ^ across) * 2 + core))
        return lax.ppermute(value, "dp", pairs)

    def to_twin(value):
        return lax.ppermute(value, "dp", [(i, i ^ 1) for i in range(count)])

    vmem = pl.BlockSpec(memory_space=pltpu.VMEM)
    hbm = pl.BlockSpec(memory_space=pl.ANY)
    smem = pl.BlockSpec(memory_space=pltpu.SMEM)
    turned = pltpu.VMEM((HG, HD, TILE), BF16)
    stats_shape = jax.ShapeDtypeStruct((slots, 8, TILE), F32)
    product = 2 * QH * TILE * TILE * HD * per_device

    def cost(products_done):
        return pl.CostEstimate(flops=3 * products_done * product, bytes_accessed=2**23, transcendentals=0)

    chip = jnp.concatenate([kv_cache, to_twin(kv_cache)], axis=0)
    arrived = [send(chip, number, True) for number in range(len(ROUNDS))]
    own_stats = pl.pallas_call(
        functools.partial(own_stats_kernel, per_device),
        out_shape=stats_shape,
        in_specs=[smem, hbm, vmem, vmem],
        out_specs=vmem,
        scratch_shapes=[pltpu.VMEM((chip_rows, 2 * HD), BF16), turned, turned, pltpu.SemaphoreType.DMA((2,))],
        compiler_params=pltpu.CompilerParams(vmem_limit_bytes=24 * 2**20),
        cost_estimate=cost(8),
        name="own_stats",
    )(pair_lengths, chip, queries, grad_out)

    arrived = [lax.optimization_barrier((rows, own_stats))[0] for rows in arrived]
    passed = jax.ShapeDtypeStruct((chip_rows, 2 * HD), BF16)
    dq_far, stats, *partial = pl.pallas_call(
        functools.partial(far_kernel, per_device),
        out_shape=(jax.ShapeDtypeStruct((slots, HD, TILE), F32), stats_shape) + (passed,) * 6,
        in_specs=[smem] + [hbm] * 6 + [vmem, vmem, vmem],
        out_specs=(vmem, vmem) + (hbm,) * 6,
        scratch_shapes=[
            pltpu.VMEM((far_rows, 2 * HD), BF16),
            pltpu.VMEM((far_rows, 2 * HD), F32),
            pltpu.VMEM((far_rows, 2 * HD), BF16),
            pltpu.VMEM((HG, (MOST - 1) * TILE, TILE), F32),
            pltpu.VMEM((HG, (MOST - 1) * TILE, TILE), F32),
            pltpu.VMEM((HG, MOST, 1, TILE), F32),
            pltpu.VMEM((HD, MOST * TILE), BF16),
            turned,
            turned,
            pltpu.SemaphoreType.DMA((2, len(ROUNDS), 2)),
            pltpu.SemaphoreType.DMA((2, len(ROUNDS), 2)),
        ],
        compiler_params=pltpu.CompilerParams(vmem_limit_bytes=44 * 2**20),
        cost_estimate=cost(40),
        name="far",
    )(pair_lengths, *arrived, *[to_twin(rows) for rows in arrived], queries, grad_out, own_stats)

    landed = []
    for number in range(len(ROUNDS)):
        both = partial[number].astype(F32) + to_twin(partial[len(ROUNDS) + number]).astype(F32)
        landed.append(send(both.astype(BF16), number, False))
    grad_queries, own_grad = pl.pallas_call(
        functools.partial(own_grads_kernel, per_device),
        out_shape=(
            jax.ShapeDtypeStruct(queries.shape, BF16),
            jax.ShapeDtypeStruct((chip_rows, 2 * HD), F32),
        ),
        in_specs=[smem, hbm, vmem, vmem, vmem, vmem],
        out_specs=(vmem, hbm),
        scratch_shapes=[
            pltpu.VMEM((chip_rows, 2 * HD), BF16),
            pltpu.VMEM((chip_rows, 2 * HD), F32),
            pltpu.VMEM((2 * per_device, HD, TILE), BF16),
            turned,
            turned,
            pltpu.VMEM((HG, HD, TILE), F32),
            pltpu.SemaphoreType.DMA((2,)),
            pltpu.SemaphoreType.DMA((2,)),
        ],
        compiler_params=pltpu.CompilerParams(vmem_limit_bytes=32 * 2**20),
        cost_estimate=cost(20),
        name="own_grads",
    )(pair_lengths, chip, queries, grad_out, stats, dq_far)
    total = own_grad
    for part in landed:
        total = total + part.astype(F32)
    grad_kv = total[:rows_dev] + to_twin(total[rows_dev:].astype(BF16)).astype(F32)
    return grad_queries, grad_kv


def solution(mesh):
    tokens = P(("groups", "dp"), None)
    return jax.shard_map(
        body,
        mesh=mesh,
        in_specs=(tokens, tokens, tokens, P("groups")),
        out_specs=(tokens, tokens),
        check_vma=False,
    )
```

```python
import functools

import jax
import jax.numpy as jnp
from jax import lax
from jax.experimental import pallas as pl
from jax.experimental.pallas import tpu as pltpu
from jax.sharding import PartitionSpec as P

HD = 128
QH = 8
HG = 4
TILE = 256
MOST = 12
FAR_STEPS = (8, 2, 1)
OWN_STEPS = (4, 2, 1)
REACH = 3
SCALE = HD**-0.5
SCALE_LOG2 = SCALE * 1.4426950408889634
F32 = jnp.float32
BF16 = jnp.bfloat16
GROUPS = QH // HG

ROUNDS = (("row", "near_across"), ("far_across", "two_rows"), ("up", "down"))
SHORT = 1


def chip_step(relation, column):
    return {
        "row": 1 - 2 * column,
        "up": 2,
        "down": -2,
        "near_across": 2 * column - 1,
        "far_across": 3 - 6 * column,
        "two_rows": 6 * column - 3,
    }[relation]


def grid_step(relation, column):
    return {
        "row": (0, 1),
        "up": (1, 0),
        "down": (-1, 0),
        "near_across": (2 * column - 1, 1),
        "far_across": (1 - 2 * column, 1),
        "two_rows": (4 * column - 2, 1),
    }[relation]


class Place:
    def __init__(self, lengths, per_device, index):
        me = lax.axis_index("dp")
        per_chip = 2 * per_device
        tile = index // GROUPS
        self.group = index % GROUPS
        own_tile = me * per_device + tile
        first = jnp.int32(0)
        last = jnp.int32(0)
        end = jnp.int32(0)
        for pair in range(lengths.shape[0]):
            start = end
            end = start + lengths[pair]
            inside = (own_tile >= start) & (own_tile < end)
            first = jnp.where(inside, start, first)
            last = jnp.where(inside, end, last)
        chip_start = (me // 2) * per_chip
        chip_end = chip_start + per_chip
        below = jnp.maximum(chip_start - first, 0)
        above = jnp.maximum(last - chip_end, 0)
        self.far_base = REACH * per_chip - below
        self.far_count = below + above
        self.own_base = jnp.maximum(first, chip_start) - chip_start
        self.own_count = jnp.minimum(last, chip_end) - chip_start - self.own_base
        self.rows = pl.ds(pl.multiple_of(tile * TILE, TILE), TILE)
        self.slot = tile * QH + self.group * HG

    def cols(self, head):
        return pl.ds(pl.multiple_of((self.group * HG + head) * HD, HD), HD)


def tiles(block, blocks):
    return pl.ds(pl.multiple_of(block * TILE, TILE), blocks * TILE)


def sweep(count, sizes, step, state):
    done = 0
    for size in sizes:
        rounds = (count - done) // size
        state = lax.fori_loop(0, rounds, lambda i, s, d=done, n=size: step(d + i * n, n, s), state)
        done = done + rounds * size
    return state


def products(place, kv, at, q_t, g_t, head):
    score = jnp.dot(kv[at, :HD], q_t[head], preferred_element_type=F32)
    gprob = jnp.dot(kv[at, HD:], g_t[head], preferred_element_type=F32)
    return score, gprob


def gathered(state, score, gprob):
    top, total, weighted = state
    new_top = jnp.maximum(top, jnp.max(score, axis=0, keepdims=True))
    weight = jnp.exp2((score - new_top) * SCALE_LOG2)
    fade = jnp.exp2((top - new_top) * SCALE_LOG2)
    total = total * fade + jnp.sum(weight, axis=0, keepdims=True)
    weighted = weighted * fade + jnp.sum(weight * gprob, axis=0, keepdims=True)
    return (new_top, total, weighted), weight


def turn_rows(place, q_ref, g_ref, q_t, g_t):
    for head in range(HG):
        q_t[head] = q_ref[place.rows, place.cols(head)].T
        g_t[head] = g_ref[place.rows, place.cols(head)].T


def own_stats_kernel(per_device, lengths, kv, q_ref, g_ref, stats_ref, q_t, g_t):
    def unit(index, _):
        place = Place(lengths, per_device, index)
        turn_rows(place, q_ref, g_ref, q_t, g_t)

        def step(block, blocks, state):
            at = tiles(place.own_base + block, blocks)
            return tuple(
                gathered(state[head], *products(place, kv, at, q_t, g_t, head))[0] for head in range(HG)
            )

        zero = jnp.zeros((1, TILE), F32)
        start = tuple((jnp.full((1, TILE), -jnp.inf, F32), zero, zero) for _ in range(HG))
        state = sweep(place.own_count, OWN_STEPS, step, start)
        for head in range(HG):
            for row in range(3):
                stats_ref[place.slot + head, row : row + 1] = state[head][row]
        return 0

    lax.fori_loop(0, per_device * GROUPS, unit, 0)


def far_kernel(
    per_device, lengths, mine_0, mine_1, mine_2, twin_0, twin_1, twin_2, q_ref, g_ref, stats_in,
    dq_out, stats_ref, mine_out_0, mine_out_1, mine_out_2, twin_out_0, twin_out_1, twin_out_2, kv, acc, low, exps, gprobs, maxes, keys_t, q_t, g_t, dq_ref, in_sems, out_sems, dq_sems,
):
    per_chip = 2 * per_device
    me = lax.axis_index("dp")
    core = lax.rem(me, 2)
    column = lax.rem(me // 2, 2)

    def near(number, carrier):
        steps = [chip_step(relation, column) for relation in ROUNDS[number]]
        step = jnp.where(carrier == 0, steps[0], steps[1])
        tile = jnp.where(step < 0, step + REACH, step + REACH - 1) * per_chip
        if number == SHORT:
            return tiles(tile + jnp.where(step < 0, 1, 0), per_chip - 1)
        return tiles(tile, per_chip)

    arrived = ((mine_0, mine_1, mine_2), (twin_0, twin_1, twin_2))
    leaving = ((mine_out_0, mine_out_1, mine_out_2), (twin_out_0, twin_out_1, twin_out_2))
    loads = []
    for number in range(len(ROUNDS)):
        for side, carrier in enumerate((core, 1 - core)):
            loads.append(
                pltpu.make_async_copy(
                    arrived[side][number], kv.at[near(number, carrier)], in_sems.at[side, number]
                )
            )
            loads[-1].start()
    acc[...] = jnp.zeros_like(acc)
    for load in loads:
        load.wait()

    def unit(index, _):
        place = Place(lengths, per_device, index)

        @pl.when(place.group == 0)
        def _():
            def turn(block, _):
                keys_t[:, tiles(block, 1)] = kv[tiles(place.far_base + block, 1), :HD].T
                return 0

            lax.fori_loop(0, place.far_count, turn, 0)

        turn_rows(place, q_ref, g_ref, q_t, g_t)

        def scores(block, blocks, state):
            at, here = tiles(place.far_base + block, blocks), tiles(block, blocks)
            done = []
            for head in range(HG):
                score, gprob = products(place, kv, at, q_t, g_t, head)
                gprobs[head, here] = gprob
                after, weight = gathered(state[head], score, gprob)
                exps[head, here] = weight
                maxes[head, block] = after[0]
                done.append(after)
            return tuple(done)

        start = tuple(
            tuple(stats_in[place.slot + head, row : row + 1] for row in range(3)) for head in range(HG)
        )
        state = sweep(place.far_count, FAR_STEPS, scores, start)
        stats = tuple((top, 1.0 / total, weighted / total) for top, total, weighted in state)
        for head in range(HG):
            top, total, weighted = state[head]
            stats_ref[place.slot + head, 0:1] = top * SCALE_LOG2 + jnp.log2(total)
            stats_ref[place.slot + head, 1:2] = weighted / total
            dq_ref[place.slot + head] = jnp.zeros((HD, TILE), F32)

        def grads(block, blocks, _):
            at, here = tiles(place.far_base + block, blocks), tiles(block, blocks)
            key_t = keys_t[:, here]
            for head in range(HG):
                top, inverse, delta = stats[head]
                factor = jnp.exp2((maxes[head, block] - top) * SCALE_LOG2) * inverse
                prob = exps[head, here] * factor
                dscore = (prob * (gprobs[head, here] - delta)).astype(BF16)
                prob = prob.astype(BF16)
                dq_ref[place.slot + head] += jnp.dot(key_t, dscore, preferred_element_type=F32)
                acc[at, :HD] += SCALE * jnp.dot(
                    dscore, q_ref[place.rows, place.cols(head)], preferred_element_type=F32
                )
                acc[at, HD:] += jnp.dot(prob, g_ref[place.rows, place.cols(head)], preferred_element_type=F32)
            return 0

        sweep(place.far_count, FAR_STEPS, grads, 0)
        dq_copy(index).start()
        return 0

    def dq_copy(index):
        at = pl.ds(index * HG, HG)
        return pltpu.make_async_copy(dq_ref.at[at], dq_out.at[at], dq_sems.at[index])

    lax.fori_loop(0, per_device * GROUPS, unit, 0)

    low[...] = acc[...].astype(BF16)
    stores = []
    for number in range(len(ROUNDS)):
        for side, carrier in enumerate((core, 1 - core)):
            stores.append(
                pltpu.make_async_copy(
                    low.at[near(number, carrier)], leaving[side][number], out_sems.at[side, number]
                )
            )
            stores[-1].start()
    for index in range(per_device * GROUPS):
        dq_copy(index).wait()
    for store in stores:
        store.wait()


def own_grads_kernel(
    per_device, lengths, kv, q_ref, g_ref, stats_ref, dq_in, dq_ref, acc, keys_t, q_t, g_t, dq_t
):
    acc[...] = jnp.zeros_like(acc)
    for block in range(2 * per_device):
        keys_t[block] = kv[block * TILE : (block + 1) * TILE, :HD].T

    def unit(index, _):
        place = Place(lengths, per_device, index)
        turn_rows(place, q_ref, g_ref, q_t, g_t)
        for head in range(HG):
            dq_t[head] = dq_in[place.slot + head]

        def grads(block, blocks, _):
            at = tiles(place.own_base + block, blocks)
            for head in range(HG):
                score, gprob = products(place, kv, at, q_t, g_t, head)
                prob = jnp.exp2(score * SCALE_LOG2 - stats_ref[place.slot + head, 0:1])
                dscore = (prob * (gprob - stats_ref[place.slot + head, 1:2])).astype(BF16)
                prob = prob.astype(BF16)
                dq = dq_t[head]
                for turn in range(blocks):
                    dq = dq + jnp.dot(
                        keys_t[place.own_base + block + turn],
                        dscore[turn * TILE : (turn + 1) * TILE],
                        preferred_element_type=F32,
                    )
                dq_t[head] = dq
                acc[at, :HD] += SCALE * jnp.dot(
                    dscore, q_ref[place.rows, place.cols(head)], preferred_element_type=F32
                )
                acc[at, HD:] += jnp.dot(prob, g_ref[place.rows, place.cols(head)], preferred_element_type=F32)
            return 0

        sweep(place.own_count, OWN_STEPS, grads, 0)
        for head in range(HG):
            dq_ref[place.rows, place.cols(head)] = (dq_t[head] * SCALE).T.astype(BF16)
        return 0

    lax.fori_loop(0, per_device * GROUPS, unit, 0)


def body(queries, kv_cache, grad_out, pair_lengths):
    rows_dev = queries.shape[0]
    per_device = rows_dev // TILE
    assert 2 * per_device * REACH >= MOST
    count = lax.axis_size("dp")
    chip_rows = 2 * rows_dev
    far_rows = 2 * REACH * chip_rows
    slots = per_device * QH

    def send(value, number, back):
        pairs = []
        for source in range(count):
            row, column, core = source // 4, (source // 2) % 2, source % 2
            relation = ROUNDS[number][core]
            rows, across = grid_step(relation, column)
            if back and relation in ("up", "down"):
                rows = -rows
            if 0 <= row + rows < count // 4:
                pairs.append((source, (row + rows) * 4 + (column ^ across) * 2 + core))
        return lax.ppermute(value, "dp", pairs)

    def to_twin(value):
        return lax.ppermute(value, "dp", [(i, i ^ 1) for i in range(count)])

    vmem = pl.BlockSpec(memory_space=pltpu.VMEM)
    hbm = pl.BlockSpec(memory_space=pl.ANY)
    smem = pl.BlockSpec(memory_space=pltpu.SMEM)
    turned = pltpu.VMEM((HG, HD, TILE), BF16)
    stats_shape = jax.ShapeDtypeStruct((slots, 8, TILE), F32)
    product = 2 * QH * TILE * TILE * HD * per_device

    def cost(products_done):
        return pl.CostEstimate(flops=3 * products_done * product, bytes_accessed=2**23, transcendentals=0)

    me = lax.axis_index("dp")
    core, column = me & 1, (me >> 1) & 1
    skipped = jnp.where(core == column, TILE, 0)
    short_rows = chip_rows - TILE
    chip = lax.dynamic_slice_in_dim(
        jnp.concatenate([kv_cache, to_twin(kv_cache), kv_cache], axis=0), core * rows_dev, chip_rows, 0
    )
    short = lax.dynamic_slice_in_dim(chip, skipped, short_rows, 0)
    arrived = [send(short if number == SHORT else chip, number, True) for number in range(len(ROUNDS))]
    own_stats = pl.pallas_call(
        functools.partial(own_stats_kernel, per_device),
        out_shape=stats_shape,
        in_specs=[smem, vmem, vmem, vmem],
        out_specs=vmem,
        scratch_shapes=[turned, turned],
        compiler_params=pltpu.CompilerParams(vmem_limit_bytes=24 * 2**20),
        cost_estimate=cost(8),
        name="own_stats",
    )(pair_lengths, chip, queries, grad_out)

    arrived = [lax.optimization_barrier((rows, own_stats))[0] for rows in arrived]
    passed = tuple(jax.ShapeDtypeStruct(rows.shape, BF16) for rows in arrived)
    dq_far, stats, *partial = pl.pallas_call(
        functools.partial(far_kernel, per_device),
        out_shape=(pltpu.HBM((slots, HD, TILE), F32), stats_shape) + passed + passed,
        in_specs=[smem] + [hbm] * 6 + [vmem, vmem, vmem],
        out_specs=(pl.BlockSpec(memory_space=pltpu.HBM), vmem) + (hbm,) * 6,
        scratch_shapes=[
            pltpu.VMEM((far_rows, 2 * HD), BF16),
            pltpu.VMEM((far_rows, 2 * HD), F32),
            pltpu.VMEM((far_rows, 2 * HD), BF16),
            pltpu.VMEM((HG, (MOST - 1) * TILE, TILE), F32),
            pltpu.VMEM((HG, (MOST - 1) * TILE, TILE), F32),
            pltpu.VMEM((HG, MOST, 1, TILE), F32),
            pltpu.VMEM((HD, MOST * TILE), BF16),
            turned,
            turned,
            pltpu.VMEM((slots, HD, TILE), F32),
            pltpu.SemaphoreType.DMA((2, len(ROUNDS))),
            pltpu.SemaphoreType.DMA((2, len(ROUNDS))),
            pltpu.SemaphoreType.DMA((per_device * GROUPS,)),
        ],
        compiler_params=pltpu.CompilerParams(vmem_limit_bytes=43 * 2**20),
        cost_estimate=cost(40),
        name="far",
    )(pair_lengths, *arrived, *[to_twin(rows) for rows in arrived], queries, grad_out, own_stats)

    landed = []
    for number in range(len(ROUNDS)):
        both = partial[number].astype(F32) + to_twin(partial[len(ROUNDS) + number]).astype(F32)
        landed.append(send(both.astype(BF16), number, False))
    grad_queries, own_grad = pl.pallas_call(
        functools.partial(own_grads_kernel, per_device),
        out_shape=(
            jax.ShapeDtypeStruct(queries.shape, BF16),
            jax.ShapeDtypeStruct((chip_rows, 2 * HD), F32),
        ),
        in_specs=[smem, vmem, vmem, vmem, vmem, vmem],
        out_specs=(vmem, vmem),
        scratch_shapes=[
            pltpu.VMEM((2 * per_device, HD, TILE), BF16),
            turned,
            turned,
            pltpu.VMEM((HG, HD, TILE), F32),
        ],
        compiler_params=pltpu.CompilerParams(vmem_limit_bytes=32 * 2**20),
        cost_estimate=cost(20),
        name="own_grads",
    )(pair_lengths, chip, queries, grad_out, stats, dq_far)
    total = own_grad
    for number, part in enumerate(landed):
        if number == SHORT:
            part = jnp.pad(part, ((TILE, TILE), (0, 0)))
            part = lax.dynamic_slice_in_dim(part, TILE - skipped, chip_rows, 0)
        total = total + part.astype(F32)
    own_rows = lax.dynamic_slice_in_dim(total, core * rows_dev, rows_dev, 0)
    twin_rows = lax.dynamic_slice_in_dim(total, (1 - core) * rows_dev, rows_dev, 0)
    grad_kv = own_rows + to_twin(twin_rows.astype(BF16)).astype(F32)
    return grad_queries, grad_kv


def solution(mesh):
    tokens = P(("groups", "dp"), None)
    return jax.shard_map(
        body,
        mesh=mesh,
        in_specs=(tokens, tokens, tokens, P("groups")),
        out_specs=(tokens, tokens),
        check_vma=False,
    )
```

```python
import functools

import jax
import jax.numpy as jnp
from jax import lax
from jax.experimental import pallas as pl
from jax.experimental.pallas import tpu as pltpu
from jax.sharding import PartitionSpec as P

HD = 128
QH = 8
HG = 4
TILE = 256
MOST = 12
FAR_STEPS = (8, 2, 1)
OWN_STEPS = (4, 2, 1)
REACH = 3
SCALE = HD**-0.5
SCALE_LOG2 = SCALE * 1.4426950408889634
F32 = jnp.float32
BF16 = jnp.bfloat16
GROUPS = QH // HG

ROUNDS = (("row", "near_across"), ("far_across", "two_rows"), ("up", "down"))
SHORT = 1


def chip_step(relation, column):
    return {
        "row": 1 - 2 * column,
        "up": 2,
        "down": -2,
        "near_across": 2 * column - 1,
        "far_across": 3 - 6 * column,
        "two_rows": 6 * column - 3,
    }[relation]


def grid_step(relation, column):
    return {
        "row": (0, 1),
        "up": (1, 0),
        "down": (-1, 0),
        "near_across": (2 * column - 1, 1),
        "far_across": (1 - 2 * column, 1),
        "two_rows": (4 * column - 2, 1),
    }[relation]


class Place:
    def __init__(self, lengths, per_device, index):
        me = lax.axis_index("dp")
        per_chip = 2 * per_device
        tile = index // GROUPS
        self.group = index % GROUPS
        own_tile = me * per_device + tile
        first = jnp.int32(0)
        last = jnp.int32(0)
        end = jnp.int32(0)
        for pair in range(lengths.shape[0]):
            start = end
            end = start + lengths[pair]
            inside = (own_tile >= start) & (own_tile < end)
            first = jnp.where(inside, start, first)
            last = jnp.where(inside, end, last)
        chip_start = (me // 2) * per_chip
        chip_end = chip_start + per_chip
        below = jnp.maximum(chip_start - first, 0)
        above = jnp.maximum(last - chip_end, 0)
        self.far_base = REACH * per_chip - below
        self.far_count = below + above
        self.own_base = jnp.maximum(first, chip_start) - chip_start
        self.own_count = jnp.minimum(last, chip_end) - chip_start - self.own_base
        self.rows = pl.ds(pl.multiple_of(tile * TILE, TILE), TILE)
        self.slot = tile * QH + self.group * HG

    def cols(self, head):
        return pl.ds(pl.multiple_of((self.group * HG + head) * HD, HD), HD)


def tiles(block, blocks):
    return pl.ds(pl.multiple_of(block * TILE, TILE), blocks * TILE)


def sweep(count, sizes, step, state):
    done = 0
    for size in sizes:
        rounds = (count - done) // size
        state = lax.fori_loop(0, rounds, lambda i, s, d=done, n=size: step(d + i * n, n, s), state)
        done = done + rounds * size
    return state


def products(place, kv, at, q_t, g_t, head):
    score = jnp.dot(kv[at, :HD], q_t[head], preferred_element_type=F32)
    gprob = jnp.dot(kv[at, HD:], g_t[head], preferred_element_type=F32)
    return score, gprob


def gathered(state, score, gprob):
    top, total, weighted = state
    new_top = jnp.maximum(top, jnp.max(score, axis=0, keepdims=True))
    weight = jnp.exp2((score - new_top) * SCALE_LOG2)
    fade = jnp.exp2((top - new_top) * SCALE_LOG2)
    total = total * fade + jnp.sum(weight, axis=0, keepdims=True)
    weighted = weighted * fade + jnp.sum(weight * gprob, axis=0, keepdims=True)
    return (new_top, total, weighted), weight


def turn_rows(place, q_ref, g_ref, q_t, g_t):
    for head in range(HG):
        q_t[head] = q_ref[place.rows, place.cols(head)].T
        g_t[head] = g_ref[place.rows, place.cols(head)].T


def own_stats_kernel(per_device, lengths, kv, q_ref, g_ref, stats_ref, q_t, g_t):
    def unit(index, _):
        place = Place(lengths, per_device, index)
        turn_rows(place, q_ref, g_ref, q_t, g_t)

        def step(block, blocks, state):
            at = tiles(place.own_base + block, blocks)
            return tuple(
                gathered(state[head], *products(place, kv, at, q_t, g_t, head))[0] for head in range(HG)
            )

        zero = jnp.zeros((1, TILE), F32)
        start = tuple((jnp.full((1, TILE), -jnp.inf, F32), zero, zero) for _ in range(HG))
        state = sweep(place.own_count, OWN_STEPS, step, start)
        for head in range(HG):
            for row in range(3):
                stats_ref[place.slot + head, row : row + 1] = state[head][row]
        return 0

    lax.fori_loop(0, per_device * GROUPS, unit, 0)


def far_kernel(
    per_device, lengths, mine_0, mine_1, mine_2, twin_0, twin_1, twin_2, q_ref, g_ref, stats_in,
    dq_out, stats_ref, mine_out_0, mine_out_1, mine_out_2, twin_out_0, twin_out_1, twin_out_2, kv, acc, low, exps, gprobs, maxes, keys_t, q_t, g_t, dq_ref, in_sems, out_sems, dq_sems,
):
    per_chip = 2 * per_device
    me = lax.axis_index("dp")
    core = lax.rem(me, 2)
    column = lax.rem(me // 2, 2)

    def near(number, carrier):
        steps = [chip_step(relation, column) for relation in ROUNDS[number]]
        step = jnp.where(carrier == 0, steps[0], steps[1])
        tile = jnp.where(step < 0, step + REACH, step + REACH - 1) * per_chip
        if number == SHORT:
            return tiles(tile + jnp.where(step < 0, 1, 0), per_chip - 1)
        return tiles(tile, per_chip)

    arrived = ((mine_0, mine_1, mine_2), (twin_0, twin_1, twin_2))
    leaving = ((mine_out_0, mine_out_1, mine_out_2), (twin_out_0, twin_out_1, twin_out_2))
    loads = []
    for number in range(len(ROUNDS)):
        for side, carrier in enumerate((core, 1 - core)):
            loads.append(
                pltpu.make_async_copy(
                    arrived[side][number], kv.at[near(number, carrier)], in_sems.at[side, number]
                )
            )
            loads[-1].start()
    acc[...] = jnp.zeros_like(acc)
    for load in loads:
        load.wait()

    def unit(index, _):
        place = Place(lengths, per_device, index)

        @pl.when(place.group == 0)
        def _():
            def turn(block, _):
                keys_t[:, tiles(block, 1)] = kv[tiles(place.far_base + block, 1), :HD].T
                return 0

            lax.fori_loop(0, place.far_count, turn, 0)

        turn_rows(place, q_ref, g_ref, q_t, g_t)

        def scores(block, blocks, state):
            at, here = tiles(place.far_base + block, blocks), tiles(block, blocks)
            done = []
            for head in range(HG):
                score, gprob = products(place, kv, at, q_t, g_t, head)
                gprobs[head, here] = gprob
                after, weight = gathered(state[head], score, gprob)
                exps[head, here] = weight
                maxes[head, block] = after[0]
                done.append(after)
            return tuple(done)

        start = tuple(
            tuple(stats_in[place.slot + head, row : row + 1] for row in range(3)) for head in range(HG)
        )
        state = sweep(place.far_count, FAR_STEPS, scores, start)
        stats = tuple((top, 1.0 / total, weighted / total) for top, total, weighted in state)
        for head in range(HG):
            top, total, weighted = state[head]
            stats_ref[place.slot + head, 0:1] = top * SCALE_LOG2 + jnp.log2(total)
            stats_ref[place.slot + head, 1:2] = weighted / total
            dq_ref[place.slot + head] = jnp.zeros((HD, TILE), F32)

        def grads(block, blocks, _):
            at, here = tiles(place.far_base + block, blocks), tiles(block, blocks)
            key_t = keys_t[:, here]
            for head in range(HG):
                top, inverse, delta = stats[head]
                factor = jnp.exp2((maxes[head, block] - top) * SCALE_LOG2) * inverse
                prob = exps[head, here] * factor
                dscore = (prob * (gprobs[head, here] - delta)).astype(BF16)
                prob = prob.astype(BF16)
                dq_ref[place.slot + head] += jnp.dot(key_t, dscore, preferred_element_type=F32)
                acc[at, :HD] += SCALE * jnp.dot(
                    dscore, q_ref[place.rows, place.cols(head)], preferred_element_type=F32
                )
                acc[at, HD:] += jnp.dot(prob, g_ref[place.rows, place.cols(head)], preferred_element_type=F32)
            return 0

        sweep(place.far_count, FAR_STEPS, grads, 0)
        dq_copy(index).start()
        return 0

    def dq_copy(index):
        at = pl.ds(index * HG, HG)
        return pltpu.make_async_copy(dq_ref.at[at], dq_out.at[at], dq_sems.at[index])

    lax.fori_loop(0, per_device * GROUPS, unit, 0)

    low[...] = acc[...].astype(BF16)
    stores = []
    for number in range(len(ROUNDS)):
        for side, carrier in enumerate((core, 1 - core)):
            stores.append(
                pltpu.make_async_copy(
                    low.at[near(number, carrier)], leaving[side][number], out_sems.at[side, number]
                )
            )
            stores[-1].start()
    for index in range(per_device * GROUPS):
        dq_copy(index).wait()
    for store in stores:
        store.wait()


def own_grads_kernel(
    per_device, tile, lengths, kv, q_ref, g_ref, stats_ref, dq_in, *rest
):
    if tile == 0:
        dq_ref, acc, keys_t, q_t, g_t, dq_t = rest
        acc[...] = jnp.zeros_like(acc)
    else:
        acc_in, _, dq_ref, acc, keys_t, q_t, g_t, dq_t = rest
        acc[...] = acc_in[...]
    for block in range(2 * per_device):
        keys_t[block] = kv[block * TILE : (block + 1) * TILE, :HD].T

    def unit(index, _):
        place = Place(lengths, per_device, tile * GROUPS + index)
        place.rows = pl.ds(0, TILE)
        place.slot = index * HG
        turn_rows(place, q_ref, g_ref, q_t, g_t)
        for head in range(HG):
            dq_t[head] = dq_in[place.slot + head]

        def grads(block, blocks, _):
            at = tiles(place.own_base + block, blocks)
            for head in range(HG):
                score, gprob = products(place, kv, at, q_t, g_t, head)
                prob = jnp.exp2(score * SCALE_LOG2 - stats_ref[place.slot + head, 0:1])
                dscore = (prob * (gprob - stats_ref[place.slot + head, 1:2])).astype(BF16)
                prob = prob.astype(BF16)
                dq = dq_t[head]
                for turn in range(blocks):
                    dq = dq + jnp.dot(
                        keys_t[place.own_base + block + turn],
                        dscore[turn * TILE : (turn + 1) * TILE],
                        preferred_element_type=F32,
                    )
                dq_t[head] = dq
                acc[at, :HD] += SCALE * jnp.dot(
                    dscore, q_ref[place.rows, place.cols(head)], preferred_element_type=F32
                )
                acc[at, HD:] += jnp.dot(prob, g_ref[place.rows, place.cols(head)], preferred_element_type=F32)
            return 0

        sweep(place.own_count, OWN_STEPS, grads, 0)
        for head in range(HG):
            dq_ref[place.rows, place.cols(head)] = (dq_t[head] * SCALE).T.astype(BF16)
        return 0

    lax.fori_loop(0, GROUPS, unit, 0)


def body(queries, kv_cache, grad_out, pair_lengths):
    rows_dev = queries.shape[0]
    per_device = rows_dev // TILE
    assert 2 * per_device * REACH >= MOST
    count = lax.axis_size("dp")
    chip_rows = 2 * rows_dev
    far_rows = 2 * REACH * chip_rows
    slots = per_device * QH

    def send(value, number, back):
        pairs = []
        for source in range(count):
            row, column, core = source // 4, (source // 2) % 2, source % 2
            relation = ROUNDS[number][core]
            rows, across = grid_step(relation, column)
            if back and relation in ("up", "down"):
                rows = -rows
            if 0 <= row + rows < count // 4:
                pairs.append((source, (row + rows) * 4 + (column ^ across) * 2 + core))
        return lax.ppermute(value, "dp", pairs)

    def to_twin(value):
        return lax.ppermute(value, "dp", [(i, i ^ 1) for i in range(count)])

    vmem = pl.BlockSpec(memory_space=pltpu.VMEM)
    hbm = pl.BlockSpec(memory_space=pl.ANY)
    smem = pl.BlockSpec(memory_space=pltpu.SMEM)
    turned = pltpu.VMEM((HG, HD, TILE), BF16)
    stats_shape = jax.ShapeDtypeStruct((slots, 8, TILE), F32)
    product = 2 * QH * TILE * TILE * HD * per_device

    def cost(products_done):
        return pl.CostEstimate(flops=3 * products_done * product, bytes_accessed=2**23, transcendentals=0)

    me = lax.axis_index("dp")
    core, column = me & 1, (me >> 1) & 1
    skipped = jnp.where(core == column, TILE, 0)
    short_rows = chip_rows - TILE
    chip = lax.dynamic_slice_in_dim(
        jnp.concatenate([kv_cache, to_twin(kv_cache), kv_cache], axis=0), core * rows_dev, chip_rows, 0
    )
    short = lax.dynamic_slice_in_dim(chip, skipped, short_rows, 0)
    arrived = [send(short if number == SHORT else chip, number, True) for number in range(len(ROUNDS))]
    own_stats = pl.pallas_call(
        functools.partial(own_stats_kernel, per_device),
        out_shape=stats_shape,
        in_specs=[smem, vmem, vmem, vmem],
        out_specs=vmem,
        scratch_shapes=[turned, turned],
        compiler_params=pltpu.CompilerParams(vmem_limit_bytes=24 * 2**20),
        cost_estimate=cost(8),
        name="own_stats",
    )(pair_lengths, chip, queries, grad_out)

    arrived = [lax.optimization_barrier((rows, own_stats))[0] for rows in arrived]
    passed = tuple(jax.ShapeDtypeStruct(rows.shape, BF16) for rows in arrived)
    dq_far, stats, *partial = pl.pallas_call(
        functools.partial(far_kernel, per_device),
        out_shape=(pltpu.HBM((slots, HD, TILE), F32), stats_shape) + passed + passed,
        in_specs=[smem] + [hbm] * 6 + [vmem, vmem, vmem],
        out_specs=(pl.BlockSpec(memory_space=pltpu.HBM), vmem) + (hbm,) * 6,
        scratch_shapes=[
            pltpu.VMEM((far_rows, 2 * HD), BF16),
            pltpu.VMEM((far_rows, 2 * HD), F32),
            pltpu.VMEM((far_rows, 2 * HD), BF16),
            pltpu.VMEM((HG, (MOST - 1) * TILE, TILE), F32),
            pltpu.VMEM((HG, (MOST - 1) * TILE, TILE), F32),
            pltpu.VMEM((HG, MOST, 1, TILE), F32),
            pltpu.VMEM((HD, MOST * TILE), BF16),
            turned,
            turned,
            pltpu.VMEM((slots, HD, TILE), F32),
            pltpu.SemaphoreType.DMA((2, len(ROUNDS))),
            pltpu.SemaphoreType.DMA((2, len(ROUNDS))),
            pltpu.SemaphoreType.DMA((per_device * GROUPS,)),
        ],
        compiler_params=pltpu.CompilerParams(vmem_limit_bytes=43 * 2**20),
        cost_estimate=cost(40),
        name="far",
    )(pair_lengths, *arrived, *[to_twin(rows) for rows in arrived], queries, grad_out, own_stats)

    leaving = []
    for number in range(len(ROUNDS)):
        both = partial[number].astype(F32) + to_twin(partial[len(ROUNDS) + number]).astype(F32)
        leaving.append(both.astype(BF16))

    def own_grads(tile, stats, before):
        def rows_of(*block):
            return pl.BlockSpec(block, lambda i: (tile,) + (0,) * (len(block) - 1))

        return pl.pallas_call(
            functools.partial(own_grads_kernel, per_device, tile),
            out_shape=(
                jax.ShapeDtypeStruct(queries.shape, BF16),
                jax.ShapeDtypeStruct((chip_rows, 2 * HD), F32),
            ),
            grid=(1,),
            in_specs=[
                smem,
                vmem,
                rows_of(TILE, QH * HD),
                rows_of(TILE, QH * HD),
                rows_of(QH, 8, TILE),
                rows_of(QH, HD, TILE),
            ]
            + ([vmem, hbm] if before else []),
            out_specs=(rows_of(TILE, QH * HD), vmem),
            scratch_shapes=[
                pltpu.VMEM((2 * per_device, HD, TILE), BF16),
                turned,
                turned,
                pltpu.VMEM((HG, HD, TILE), F32),
            ],
            input_output_aliases={7: 0} if before else {},
            compiler_params=pltpu.CompilerParams(vmem_limit_bytes=32 * 2**20),
            cost_estimate=cost(10),
            name="own_grads",
        )(pair_lengths, chip, queries, grad_out, stats, dq_far, *before)

    stats, *leaving = lax.optimization_barrier((stats, *leaving))
    landed = [send(leaving[number], number, False) for number in range(len(ROUNDS) - 1)]
    grad_queries, own_grad = own_grads(0, stats, ())
    last, own_grad = lax.optimization_barrier((leaving[-1], own_grad))
    landed.append(send(last, len(ROUNDS) - 1, False))
    for tile in range(1, per_device):
        grad_queries, own_grad = own_grads(tile, stats, (own_grad, grad_queries))
    total = own_grad
    for number, part in enumerate(landed):
        if number == SHORT:
            part = jnp.pad(part, ((TILE, TILE), (0, 0)))
            part = lax.dynamic_slice_in_dim(part, TILE - skipped, chip_rows, 0)
        total = total + part.astype(F32)
    own_rows = lax.dynamic_slice_in_dim(total, core * rows_dev, rows_dev, 0)
    twin_rows = lax.dynamic_slice_in_dim(total, (1 - core) * rows_dev, rows_dev, 0)
    grad_kv = own_rows + to_twin(twin_rows.astype(BF16)).astype(F32)
    return grad_queries, grad_kv


def solution(mesh):
    tokens = P(("groups", "dp"), None)
    return jax.shard_map(
        body,
        mesh=mesh,
        in_specs=(tokens, tokens, tokens, P("groups")),
        out_specs=(tokens, tokens),
        check_vma=False,
    )
```

```python
import functools

import jax
import jax.numpy as jnp
from jax import lax
from jax.experimental import pallas as pl
from jax.experimental.pallas import tpu as pltpu
from jax.sharding import PartitionSpec as P

HD = 128
QH = 8
HG = 4
TILE = 256
MOST = 12
FAR_STEPS = (8, 2, 1)
OWN_STEPS = (4, 2, 1)
REACH = 3
SCALE = HD**-0.5
SCALE_LOG2 = SCALE * 1.4426950408889634
F32 = jnp.float32
BF16 = jnp.bfloat16
GROUPS = QH // HG

ROUNDS = (("row", "near_across"), ("far_across", "two_rows"), ("up", "down"))
SHORT = 1


def chip_step(relation, column):
    return {
        "row": 1 - 2 * column,
        "up": 2,
        "down": -2,
        "near_across": 2 * column - 1,
        "far_across": 3 - 6 * column,
        "two_rows": 6 * column - 3,
    }[relation]


def grid_step(relation, column):
    return {
        "row": (0, 1),
        "up": (1, 0),
        "down": (-1, 0),
        "near_across": (2 * column - 1, 1),
        "far_across": (1 - 2 * column, 1),
        "two_rows": (4 * column - 2, 1),
    }[relation]


class Place:
    def __init__(self, lengths, per_device, index):
        me = lax.axis_index("dp")
        per_chip = 2 * per_device
        tile = index // GROUPS
        self.group = index % GROUPS
        own_tile = me * per_device + tile
        first = jnp.int32(0)
        last = jnp.int32(0)
        end = jnp.int32(0)
        for pair in range(lengths.shape[0]):
            start = end
            end = start + lengths[pair]
            inside = (own_tile >= start) & (own_tile < end)
            first = jnp.where(inside, start, first)
            last = jnp.where(inside, end, last)
        chip_start = (me // 2) * per_chip
        chip_end = chip_start + per_chip
        below = jnp.maximum(chip_start - first, 0)
        above = jnp.maximum(last - chip_end, 0)
        self.far_base = REACH * per_chip - below
        self.far_count = below + above
        self.own_base = jnp.maximum(first, chip_start) - chip_start
        self.own_count = jnp.minimum(last, chip_end) - chip_start - self.own_base
        self.rows = pl.ds(pl.multiple_of(tile * TILE, TILE), TILE)
        self.slot = tile * QH + self.group * HG

    def cols(self, head):
        return pl.ds(pl.multiple_of((self.group * HG + head) * HD, HD), HD)


def tiles(block, blocks):
    return pl.ds(pl.multiple_of(block * TILE, TILE), blocks * TILE)


def sweep(count, sizes, step, state):
    done = 0
    for size in sizes:
        rounds = (count - done) // size
        state = lax.fori_loop(0, rounds, lambda i, s, d=done, n=size: step(d + i * n, n, s), state)
        done = done + rounds * size
    return state


def products(place, kv, at, q_t, g_t, head):
    score = jnp.dot(kv[at, :HD], q_t[head], preferred_element_type=F32)
    gprob = jnp.dot(kv[at, HD:], g_t[head], preferred_element_type=F32)
    return score, gprob


def gathered(state, score, gprob):
    top, total, weighted = state
    new_top = jnp.maximum(top, jnp.max(score, axis=0, keepdims=True))
    weight = jnp.exp2((score - new_top) * SCALE_LOG2)
    fade = jnp.exp2((top - new_top) * SCALE_LOG2)
    total = total * fade + jnp.sum(weight, axis=0, keepdims=True)
    weighted = weighted * fade + jnp.sum(weight * gprob, axis=0, keepdims=True)
    return (new_top, total, weighted), weight


def turn_rows(place, q_ref, g_ref, q_t, g_t):
    for head in range(HG):
        q_t[head] = q_ref[place.rows, place.cols(head)].T
        g_t[head] = g_ref[place.rows, place.cols(head)].T


def own_stats_kernel(per_device, lengths, kv, q_ref, g_ref, stats_ref, q_t, g_t):
    def unit(index, _):
        place = Place(lengths, per_device, index)
        turn_rows(place, q_ref, g_ref, q_t, g_t)

        def step(block, blocks, state):
            at = tiles(place.own_base + block, blocks)
            return tuple(
                gathered(state[head], *products(place, kv, at, q_t, g_t, head))[0] for head in range(HG)
            )

        zero = jnp.zeros((1, TILE), F32)
        start = tuple((jnp.full((1, TILE), -jnp.inf, F32), zero, zero) for _ in range(HG))
        state = sweep(place.own_count, OWN_STEPS, step, start)
        for head in range(HG):
            for row in range(3):
                stats_ref[place.slot + head, row : row + 1] = state[head][row]
        return 0

    lax.fori_loop(0, per_device * GROUPS, unit, 0)


def far_kernel(
    per_device, lengths, mine_0, mine_1, mine_2, twin_0, twin_1, twin_2, q_ref, g_ref, stats_in,
    dq_out, stats_out, mine_out_0, mine_out_1, mine_out_2, twin_out_0, twin_out_1, twin_out_2, kv, acc, low, exps, gprobs, maxes, keys_t, q_t, g_t, dq_ref, stats_ref, in_sems, out_sems, dq_sems, stats_sem,
):
    per_chip = 2 * per_device
    me = lax.axis_index("dp")
    core = lax.rem(me, 2)
    column = lax.rem(me // 2, 2)

    def near(number, carrier):
        steps = [chip_step(relation, column) for relation in ROUNDS[number]]
        step = jnp.where(carrier == 0, steps[0], steps[1])
        tile = jnp.where(step < 0, step + REACH, step + REACH - 1) * per_chip
        if number == SHORT:
            return tiles(tile + jnp.where(step < 0, 1, 0), per_chip - 1)
        return tiles(tile, per_chip)

    arrived = ((mine_0, mine_1, mine_2), (twin_0, twin_1, twin_2))
    leaving = ((mine_out_0, mine_out_1, mine_out_2), (twin_out_0, twin_out_1, twin_out_2))
    loads = []
    for number in range(len(ROUNDS)):
        for side, carrier in enumerate((core, 1 - core)):
            loads.append(
                pltpu.make_async_copy(
                    arrived[side][number], kv.at[near(number, carrier)], in_sems.at[side, number]
                )
            )
            loads[-1].start()
    acc[...] = jnp.zeros_like(acc)
    for load in loads:
        load.wait()

    def unit(index, _):
        place = Place(lengths, per_device, index)

        @pl.when(place.group == 0)
        def _():
            def turn(block, _):
                keys_t[:, tiles(block, 1)] = kv[tiles(place.far_base + block, 1), :HD].T
                return 0

            lax.fori_loop(0, place.far_count, turn, 0)

        turn_rows(place, q_ref, g_ref, q_t, g_t)

        def scores(block, blocks, state):
            at, here = tiles(place.far_base + block, blocks), tiles(block, blocks)
            done = []
            for head in range(HG):
                score, gprob = products(place, kv, at, q_t, g_t, head)
                gprobs[head, here] = gprob
                after, weight = gathered(state[head], score, gprob)
                exps[head, here] = weight
                maxes[head, block] = after[0]
                done.append(after)
            return tuple(done)

        start = tuple(
            tuple(stats_in[place.slot + head, row : row + 1] for row in range(3)) for head in range(HG)
        )
        state = sweep(place.far_count, FAR_STEPS, scores, start)
        stats = tuple((top, 1.0 / total, weighted / total) for top, total, weighted in state)
        for head in range(HG):
            top, total, weighted = state[head]
            stats_ref[place.slot + head, 0:1] = top * SCALE_LOG2 + jnp.log2(total)
            stats_ref[place.slot + head, 1:2] = weighted / total
            dq_ref[place.slot + head] = jnp.zeros((HD, TILE), F32)

        def grads(block, blocks, _):
            at, here = tiles(place.far_base + block, blocks), tiles(block, blocks)
            key_t = keys_t[:, here]
            for head in range(HG):
                top, inverse, delta = stats[head]
                factor = jnp.exp2((maxes[head, block] - top) * SCALE_LOG2) * inverse
                prob = exps[head, here] * factor
                dscore = (prob * (gprobs[head, here] - delta)).astype(BF16)
                prob = prob.astype(BF16)
                dq_ref[place.slot + head] += jnp.dot(key_t, dscore, preferred_element_type=F32)
                acc[at, :HD] += SCALE * jnp.dot(
                    dscore, q_ref[place.rows, place.cols(head)], preferred_element_type=F32
                )
                acc[at, HD:] += jnp.dot(prob, g_ref[place.rows, place.cols(head)], preferred_element_type=F32)
            return 0

        sweep(place.far_count, FAR_STEPS, grads, 0)
        dq_copy(index).start()
        return 0

    def dq_copy(index):
        at = pl.ds(index * HG, HG)
        return pltpu.make_async_copy(dq_ref.at[at], dq_out.at[at], dq_sems.at[index])

    lax.fori_loop(0, per_device * GROUPS, unit, 0)

    stats_copy = pltpu.make_async_copy(stats_ref, stats_out, stats_sem)
    stats_copy.start()
    low[...] = acc[...].astype(BF16)
    stores = []
    for number in range(len(ROUNDS)):
        for side, carrier in enumerate((core, 1 - core)):
            stores.append(
                pltpu.make_async_copy(
                    low.at[near(number, carrier)], leaving[side][number], out_sems.at[side, number]
                )
            )
            stores[-1].start()
    for index in range(per_device * GROUPS):
        dq_copy(index).wait()
    stats_copy.wait()
    for store in stores:
        store.wait()


def own_grads_kernel(
    per_device, tile, lengths, kv, q_ref, g_ref, stats_ref, dq_in, *rest
):
    if tile == 0:
        dq_ref, acc, keys_t, q_t, g_t, dq_t = rest
        acc[...] = jnp.zeros_like(acc)
    else:
        acc_in, _, dq_ref, acc, keys_t, q_t, g_t, dq_t = rest
        acc[...] = acc_in[...]
    for block in range(2 * per_device):
        keys_t[block] = kv[block * TILE : (block + 1) * TILE, :HD].T

    def unit(index, _):
        place = Place(lengths, per_device, tile * GROUPS + index)
        place.rows = pl.ds(0, TILE)
        place.slot = index * HG
        turn_rows(place, q_ref, g_ref, q_t, g_t)
        for head in range(HG):
            dq_t[head] = dq_in[place.slot + head]

        def grads(block, blocks, _):
            at = tiles(place.own_base + block, blocks)
            for head in range(HG):
                score, gprob = products(place, kv, at, q_t, g_t, head)
                prob = jnp.exp2(score * SCALE_LOG2 - stats_ref[place.slot + head, 0:1])
                dscore = (prob * (gprob - stats_ref[place.slot + head, 1:2])).astype(BF16)
                prob = prob.astype(BF16)
                dq = dq_t[head]
                for turn in range(blocks):
                    dq = dq + jnp.dot(
                        keys_t[place.own_base + block + turn],
                        dscore[turn * TILE : (turn + 1) * TILE],
                        preferred_element_type=F32,
                    )
                dq_t[head] = dq
                acc[at, :HD] += SCALE * jnp.dot(
                    dscore, q_ref[place.rows, place.cols(head)], preferred_element_type=F32
                )
                acc[at, HD:] += jnp.dot(prob, g_ref[place.rows, place.cols(head)], preferred_element_type=F32)
            return 0

        sweep(place.own_count, OWN_STEPS, grads, 0)
        for head in range(HG):
            dq_ref[place.rows, place.cols(head)] = (dq_t[head] * SCALE).T.astype(BF16)
        return 0

    lax.fori_loop(0, GROUPS, unit, 0)


def body(queries, kv_cache, grad_out, pair_lengths):
    rows_dev = queries.shape[0]
    per_device = rows_dev // TILE
    assert 2 * per_device * REACH >= MOST
    count = lax.axis_size("dp")
    chip_rows = 2 * rows_dev
    far_rows = 2 * REACH * chip_rows
    slots = per_device * QH

    def send(value, number, back):
        pairs = []
        for source in range(count):
            row, column, core = source // 4, (source // 2) % 2, source % 2
            relation = ROUNDS[number][core]
            rows, across = grid_step(relation, column)
            if back and relation in ("up", "down"):
                rows = -rows
            if 0 <= row + rows < count // 4:
                pairs.append((source, (row + rows) * 4 + (column ^ across) * 2 + core))
        return lax.ppermute(value, "dp", pairs)

    def to_twin(value):
        return lax.ppermute(value, "dp", [(i, i ^ 1) for i in range(count)])

    vmem = pl.BlockSpec(memory_space=pltpu.VMEM)
    hbm = pl.BlockSpec(memory_space=pl.ANY)
    smem = pl.BlockSpec(memory_space=pltpu.SMEM)
    turned = pltpu.VMEM((HG, HD, TILE), BF16)
    stats_shape = jax.ShapeDtypeStruct((slots, 8, TILE), F32)
    product = 2 * QH * TILE * TILE * HD * per_device

    def cost(products_done):
        return pl.CostEstimate(flops=3 * products_done * product, bytes_accessed=2**23, transcendentals=0)

    me = lax.axis_index("dp")
    core, column = me & 1, (me >> 1) & 1
    skipped = jnp.where(core == column, TILE, 0)
    short_rows = chip_rows - TILE
    chip = lax.dynamic_slice_in_dim(
        jnp.concatenate([kv_cache, to_twin(kv_cache), kv_cache], axis=0), core * rows_dev, chip_rows, 0
    )
    short = lax.dynamic_slice_in_dim(chip, skipped, short_rows, 0)
    arrived = [send(short if number == SHORT else chip, number, True) for number in range(len(ROUNDS))]
    own_stats = pl.pallas_call(
        functools.partial(own_stats_kernel, per_device),
        out_shape=stats_shape,
        in_specs=[smem, vmem, vmem, vmem],
        out_specs=vmem,
        scratch_shapes=[turned, turned],
        compiler_params=pltpu.CompilerParams(vmem_limit_bytes=24 * 2**20),
        cost_estimate=cost(8),
        name="own_stats",
    )(pair_lengths, chip, queries, grad_out)

    arrived = [lax.optimization_barrier((rows, own_stats))[0] for rows in arrived]
    passed = tuple(jax.ShapeDtypeStruct(rows.shape, BF16) for rows in arrived)
    dq_far, stats, *partial = pl.pallas_call(
        functools.partial(far_kernel, per_device),
        out_shape=(pltpu.HBM((slots, HD, TILE), F32), pltpu.HBM(stats_shape.shape, F32)) + passed + passed,
        in_specs=[smem] + [hbm] * 6 + [vmem, vmem, vmem],
        out_specs=(pl.BlockSpec(memory_space=pltpu.HBM),) * 2 + (hbm,) * 6,
        scratch_shapes=[
            pltpu.VMEM((far_rows, 2 * HD), BF16),
            pltpu.VMEM((far_rows, 2 * HD), F32),
            pltpu.VMEM((far_rows, 2 * HD), BF16),
            pltpu.VMEM((HG, (MOST - 1) * TILE, TILE), F32),
            pltpu.VMEM((HG, (MOST - 1) * TILE, TILE), F32),
            pltpu.VMEM((HG, MOST, 1, TILE), F32),
            pltpu.VMEM((HD, MOST * TILE), BF16),
            turned,
            turned,
            pltpu.VMEM((slots, HD, TILE), F32),
            pltpu.VMEM(stats_shape.shape, F32),
            pltpu.SemaphoreType.DMA((2, len(ROUNDS))),
            pltpu.SemaphoreType.DMA((2, len(ROUNDS))),
            pltpu.SemaphoreType.DMA((per_device * GROUPS,)),
            pltpu.SemaphoreType.DMA,
        ],
        compiler_params=pltpu.CompilerParams(vmem_limit_bytes=43 * 2**20),
        cost_estimate=cost(40),
        name="far",
    )(pair_lengths, *arrived, *[to_twin(rows) for rows in arrived], queries, grad_out, own_stats)

    leaving = []
    for number in range(len(ROUNDS)):
        both = partial[number].astype(F32) + to_twin(partial[len(ROUNDS) + number]).astype(F32)
        leaving.append(both.astype(BF16))

    def own_grads(tile, stats, before):
        def rows_of(*block):
            return pl.BlockSpec(block, lambda i: (tile,) + (0,) * (len(block) - 1))

        return pl.pallas_call(
            functools.partial(own_grads_kernel, per_device, tile),
            out_shape=(
                jax.ShapeDtypeStruct(queries.shape, BF16),
                jax.ShapeDtypeStruct((chip_rows, 2 * HD), F32),
            ),
            grid=(1,),
            in_specs=[
                smem,
                vmem,
                rows_of(TILE, QH * HD),
                rows_of(TILE, QH * HD),
                rows_of(QH, 8, TILE),
                rows_of(QH, HD, TILE),
            ]
            + ([vmem, hbm] if before else []),
            out_specs=(rows_of(TILE, QH * HD), vmem),
            scratch_shapes=[
                pltpu.VMEM((2 * per_device, HD, TILE), BF16),
                turned,
                turned,
                pltpu.VMEM((HG, HD, TILE), F32),
            ],
            input_output_aliases={7: 0} if before else {},
            compiler_params=pltpu.CompilerParams(vmem_limit_bytes=32 * 2**20),
            cost_estimate=cost(10),
            name="own_grads",
        )(pair_lengths, chip, queries, grad_out, stats, dq_far, *before)

    stats = lax.optimization_barrier((stats, *leaving[:-1]))[0]
    landed = [send(leaving[number], number, False) for number in range(len(ROUNDS) - 1)]
    grad_queries, own_grad = own_grads(0, stats, ())
    last, own_grad = lax.optimization_barrier((leaving[-1], own_grad))
    landed.append(send(last, len(ROUNDS) - 1, False))
    for tile in range(1, per_device):
        grad_queries, own_grad = own_grads(tile, stats, (own_grad, grad_queries))
    total = own_grad
    for number, part in enumerate(landed):
        if number == SHORT:
            part = jnp.pad(part, ((TILE, TILE), (0, 0)))
            part = lax.dynamic_slice_in_dim(part, TILE - skipped, chip_rows, 0)
        total = total + part.astype(F32)
    own_rows = lax.dynamic_slice_in_dim(total, core * rows_dev, rows_dev, 0)
    twin_rows = lax.dynamic_slice_in_dim(total, (1 - core) * rows_dev, rows_dev, 0)
    grad_kv = own_rows + to_twin(twin_rows.astype(BF16)).astype(F32)
    return grad_queries, grad_kv


def solution(mesh):
    tokens = P(("groups", "dp"), None)
    return jax.shard_map(
        body,
        mesh=mesh,
        in_specs=(tokens, tokens, tokens, P("groups")),
        out_specs=(tokens, tokens),
        check_vma=False,
    )
```
